128 devices in a mesh: dp: 8 (over z_lo, x), tensor: 16 (over y, z_hi, core).
Axes of the slice: x: 4, y: 4, z: 4 (z_hi: 2, z_lo: 2; z = z_hi * 2 + z_lo), core: 2. Of those that a mesh axis runs over, the one named last changes fastest.
Arguments:
- cotangent: bfloat16 [16384, 4096], P(('dp', 'tensor')), may hold values from -4 to 4
- mixer_out: bfloat16 [16384, 8192], P('dp', 'tensor'), may hold values from -60 to 60, as said below
- gate: bfloat16 [16384, 8192], P('dp', 'tensor'), may hold values from -6 to 6
- norm_gain: float32 [8192], P('tensor'), may hold values from 0.5 to 1.5
- out_weight: bfloat16 [8192, 4096], P('tensor'), may hold values from -0.0625 to 0.0625
- old_master: float32 [16, 768, 4096], P('tensor', 'dp'), may hold values from -0.3125 to 0.3125
- old_first: float32 [16, 768, 4096], P('tensor', 'dp'), may hold values from -6 to 6
- old_second: float32 [16, 768, 4096], P('tensor', 'dp'), may hold values from 0.5 to 20
- old_bounds: int32 [16, 9], P('tensor'), may hold values from 0 to 512, as said below
- new_bounds: int32 [16, 9], P('tensor'), may hold values from 0 to 512, as said below
Outputs:
- new_master: float32 [16, 768, 4096], P('tensor', 'dp')
- new_first: float32 [16, 768, 4096], P('tensor', 'dp')
- new_second: float32 [16, 768, 4096], P('tensor', 'dp')
- input_grad: bfloat16 [16384, 8192], P('dp', 'tensor')
- gate_grad: bfloat16 [16384, 8192], P('dp', 'tensor')
The draws below stay inside these ranges and needn't reach their ends.
Inputs may be any that keep to these rules, and one draw needn't show every extreme that they name: `mixer_out`: the scan's channel values. `old_bounds`: row t starts at 0, ends at 512 and never falls; old_bounds[t, j] - j * 64 lies in -16 to 0; an old share holds at most 80 rows, and in every row of the table one share holds exactly that many. `new_bounds`: row t starts at 0, ends at 512 and never falls; new_bounds[t, j] - old_bounds[t, j] lies in 0 to 16 and equals 16 for some j in every row; new_bounds[t, j] - j * 64 lies in -16 to 16, both ends reached in every row; a new share holds at most 96 rows, exactly 96 for some j in every row.
All inputs are finite; a program needn't handle non-finite values.
Results may differ from the reference program's by a relative error of at most 0.001.
Values may be sent and summed in bfloat16 or wider, within the bound.
No kernel may reach another device: no remote copies, remote signals or barrier semaphores. Data moves between devices by JAX's collectives and lax.ppermute only.
A program may use at most 192 MiB of HBM per device.

```python
import math
import jax
import jax.numpy as jnp
from jax import lax

D = 4096
INNER = 8192
GROUP = 2048
TOK = 2048
TOKENS = 16384
ROWS = 512
SHARE = 64
SPILL = 16
CAP = 96
N_DP = 8
N_TENSOR = 16


def bound_tables(key):
    key_pick, key_shift, key_spill = jax.random.split(key, 3)
    inner_count = N_DP - 1
    position = jnp.arange(inner_count, dtype=jnp.int32)[None, :]
    shift = jax.random.randint(key_shift, (N_TENSOR, inner_count), -SPILL, 1, dtype=jnp.int32)
    moved = jax.random.randint(key_spill, (N_TENSOR, inner_count), 0, SPILL + 1, dtype=jnp.int32)
    chosen = jax.random.randint(key_pick, (N_TENSOR, 1), 0, inner_count - 1, dtype=jnp.int32)
    shift = jnp.where(position == chosen, -SPILL, shift)
    moved = jnp.where(position == chosen, 0, moved)
    shift = jnp.where(position == chosen + 1, 0, shift)
    moved = jnp.where(position == chosen + 1, SPILL, moved)
    old_inner = (position + 1) * SHARE + shift
    new_inner = old_inner + moved
    first_col = jnp.zeros((N_TENSOR, 1), jnp.int32)
    last_col = jnp.full((N_TENSOR, 1), ROWS, jnp.int32)
    old_table = jnp.concatenate([first_col, old_inner, last_col], axis=1).astype(jnp.int32)
    new_table = jnp.concatenate([first_col, new_inner, last_col], axis=1).astype(jnp.int32)
    return (old_table, new_table)


def draw_old_bounds(key, part):
    old_table, new_table = bound_tables(key)
    return old_table


def draw_new_bounds(key, part):
    old_table, new_table = bound_tables(key)
    return new_table


def draw_mixer_out(key, part):
    key = jax.random.fold_in(key, 7)
    key_base, key_rough, key_rows = jax.random.split(key, 3)
    position = (jnp.arange(INNER) % GROUP).astype(jnp.float32) / GROUP
    rough = jnp.exp(jax.random.uniform(key_rough, (1, INNER), jnp.float32, -1.0, 1.0))
    base = jnp.clip(jax.random.normal(key_base, (TOKENS, INNER), jnp.float32), -4.0, 4.0)
    rising = jnp.exp(0.5 * math.log(3.0) * position)[None, :]
    row_scale = jnp.exp(jax.random.uniform(key_rows, (TOKENS, 1), jnp.float32, math.log(0.3), math.log(3.0)))
    return (base * rising * rough * row_scale).astype(jnp.bfloat16)


def block_levels(rng, shape, pieces, smallest, top_value):
    gain, own = 1.0, jax.random.fold_in(rng, 6)
    for dim, parts in pieces:
        draws = jnp.exp(jax.random.uniform(jax.random.fold_in(own, dim), (parts,), jnp.float32, smallest / len(pieces), top_value / len(pieces)))
        gain = gain * jnp.repeat(draws, shape[dim] // parts).reshape([-1 if axis == dim else 1 for axis in range(len(shape))])
    return gain


def normal_values(own_key, dims, width, most, cuts=(), kind=jnp.bfloat16):
    drawn = width * jax.random.normal(own_key, dims, jnp.float32)
    if cuts:
        drawn = drawn * block_levels(own_key, dims, cuts, -0.22, 0.18)
    return jnp.clip(drawn, -most, most).astype(kind)


def setup_inputs(seed: int = 0) -> dict:
    seeds = jax.random.split(jax.random.key(seed), 11)
    cotangent = normal_values(seeds[0], (TOKENS, D), 0.25, 4.0, ((0, 128),))
    mixer_out = draw_mixer_out(jax.random.fold_in(seeds[10], 71), 0)
    gate = normal_values(seeds[2], (TOKENS, INNER), 1.0, 6.0, ((0, 8), (1, 16)))
    norm_gain = jnp.clip(0.5 + 1.0 * jax.random.uniform(seeds[3], (INNER,), jnp.float32) ** block_levels(seeds[3], (INNER,), ((0, 16),), -0.2, 0.2), 0.5, 1.5)
    out_weight = normal_values(seeds[4], (INNER, D), INNER ** -0.5, 0.0625, ((0, 16),))
    old_master = normal_values(seeds[5], (N_TENSOR, N_DP * CAP, D), 0.02, 0.3125, ((0, 16), (1, 8)), jnp.float32)
    old_first = normal_values(seeds[6], (N_TENSOR, N_DP * CAP, D), 1.0, 6.0, ((0, 16), (1, 8)), jnp.float32)
    old_second = jnp.clip(jnp.exp(math.log(20.0) - 3.6888795 * jax.random.uniform(seeds[7], (N_TENSOR, N_DP * CAP, D), jnp.float32) ** block_levels(seeds[7], (N_TENSOR, N_DP * CAP, D), ((0, 16), (1, 8)), -0.2, 0.2)), 0.5, 20.0)
    old_bounds = draw_old_bounds(jax.random.fold_in(seeds[10], 71), 0)
    new_bounds = draw_new_bounds(jax.random.fold_in(seeds[10], 71), 0)
    return dict(cotangent=cotangent, mixer_out=mixer_out, gate=gate, norm_gain=norm_gain, out_weight=out_weight, old_master=old_master, old_first=old_first, old_second=old_second, old_bounds=old_bounds, new_bounds=new_bounds)


norm_eps = 1e-05
beta_one = 0.9
beta_two = 0.95
adam_eps = 1e-08
learn_rate = 0.0003
weight_decay = 0.1
adam_step = 1000.0

def adam_update(master, first, second, grad):
    first_new = beta_one * first + (1.0 - beta_one) * grad
    second_new = beta_two * second + (1.0 - beta_two) * grad * grad
    corr_one = 1.0 - beta_one ** adam_step
    corr_two = 1.0 - beta_two ** adam_step
    update = first_new / corr_one / (jnp.sqrt(second_new / corr_two) + adam_eps)
    return (master - learn_rate * (update + weight_decay * master), first_new, second_new)

def group_mean(values):
    token_count = values.shape[0]
    grouped = values.reshape(token_count, INNER // GROUP, GROUP)
    means = lax.optimization_barrier(jnp.mean(grouped, axis=2, keepdims=True))
    return jnp.broadcast_to(means, grouped.shape).reshape(token_count, INNER)

def reference(cotangent, mixer_out, gate, norm_gain, out_weight, old_master, old_first, old_second, old_bounds, new_bounds):

    def data_group(running, inputs):
        cot_rows, mixer_rows, gate_rows = inputs
        mixer_value = mixer_rows.astype(jnp.float32)
        gate_value = gate_rows.astype(jnp.float32)
        sigmoid_gate = jax.nn.sigmoid(gate_value)
        activated = gate_value * sigmoid_gate
        slope = sigmoid_gate * (1.0 + gate_value * (1.0 - sigmoid_gate))
        gated = mixer_value * activated
        inverse = lax.rsqrt(group_mean(gated * gated) + norm_eps)
        normed = gated * inverse
        hidden = (normed * norm_gain).astype(jnp.bfloat16)
        back = jnp.dot(cot_rows, out_weight.T, preferred_element_type=jnp.float32)
        scaled = back * norm_gain
        centre = group_mean(scaled * normed)
        gated_back = inverse * (scaled - normed * centre)
        input_rows = (gated_back * activated).astype(jnp.bfloat16)
        gate_rows_out = (gated_back * mixer_value * slope).astype(jnp.bfloat16)
        running = running + jnp.dot(hidden.T, cot_rows, preferred_element_type=jnp.float32)
        return (running, (input_rows, gate_rows_out))
    summed, (input_parts, gate_parts) = lax.scan(data_group, jnp.zeros((INNER, D), jnp.float32), (cotangent.reshape(N_DP, TOK, D), mixer_out.reshape(N_DP, TOK, INNER), gate.reshape(N_DP, TOK, INNER)))
    grad_rows = (summed / N_DP).reshape(N_TENSOR, ROWS, D)
    row_index = jnp.arange(ROWS, dtype=jnp.int32)
    inner_old = old_bounds[:, 1:N_DP]
    share_of = lax.optimization_barrier(jnp.sum((inner_old[:, None, :] <= row_index[None, :, None]).astype(jnp.int32), axis=2)).astype(jnp.int32)
    start_of = jnp.take_along_axis(old_bounds, share_of, axis=1)
    source = (share_of * CAP + row_index[None, :] - start_of).astype(jnp.int32)

    def pick(array):
        return jnp.take_along_axis(array, source[:, :, None], axis=1)
    master_rows, first_rows, second_rows = adam_update(pick(old_master), pick(old_first), pick(old_second), grad_rows)
    slot_index = jnp.arange(N_DP * CAP, dtype=jnp.int32)
    owner = jnp.broadcast_to(slot_index // CAP, (N_TENSOR, N_DP * CAP)).astype(jnp.int32)
    within = slot_index % CAP
    new_start = jnp.take_along_axis(new_bounds, owner, axis=1)
    new_end = jnp.take_along_axis(new_bounds, owner + 1, axis=1)
    valid = within[None, :] < new_end - new_start
    target = jnp.clip(new_start + within[None, :], 0, ROWS - 1).astype(jnp.int32)

    def place(array):
        return jnp.where(valid[:, :, None], jnp.take_along_axis(array, target[:, :, None], axis=1), 0.0)
    return (place(master_rows), place(first_rows), place(second_rows), input_parts.reshape(TOKENS, INNER), gate_parts.reshape(TOKENS, INNER))
```

```python
import jax
import jax.numpy as jnp
from jax import lax
from jax.experimental import pallas as pl
from jax.experimental.pallas import tpu as pltpu
from jax.sharding import PartitionSpec as P

GROUP = 2048

norm_eps = 1e-05
beta_one = 0.9
beta_two = 0.95
adam_eps = 1e-08
learn_rate = 0.0003
weight_decay = 0.1
adam_step = 1000.0

N_X, N_Y = 4, 4
AXES = ("dp", "tensor")
TILE = 1024
TOP, FINE = 32700.0, 256.0
BLOCK = 128
HALO = 16
CAP = 96
OWNERS = ((2, 1), (1, 1), (3, 1), (0, 1), (2, 0), (1, 0), (3, 0), (0, 0))
EARLY = ((0, 0), (0, 1), (3, 0), (1, 0), (2, 0))
LATE = ((3, 1), (1, 1), (2, 1))
F32 = jnp.float32
BF16 = jnp.bfloat16


def position(flat):
    dp, tensor = flat // 16, flat % 16
    return dp % 4, tensor // 4, dp // 4, (tensor // 2) % 2, tensor % 2


def flat_of(x, y, zl, zh, c):
    return (zl * 4 + x) * 16 + (y * 2 + zh) * 2 + c


def pairs_of(move):
    return [(i, flat_of(*move(*position(i)))) for i in range(128)]


TO_CORE = pairs_of(lambda x, y, zl, zh, c: (x, y, zl, zh, 1 - c))
TO_ZHI = pairs_of(lambda x, y, zl, zh, c: (x, y, zl, 1 - zh, c))
TO_YP = pairs_of(lambda x, y, zl, zh, c: (x, (y + 1) % N_Y, zl, zh, c))
TO_YM = pairs_of(lambda x, y, zl, zh, c: (x, (y - 1) % N_Y, zl, zh, c))
TO_OWNER = [pairs_of(lambda x, y, zl, zh, c: ((x + dx) % N_X, y, (zl + dz) % 2, zh, c)) for dx, dz in OWNERS]
TO_NEXT = [(i, i + 16) for i in range(112)]
TO_LAST = [(i + 16, i) for i in range(112)]


def move(value, pairs):
    return lax.ppermute(value, AXES, pairs)


def params(mib):
    return pltpu.CompilerParams(vmem_limit_bytes=mib * 2**20)


SMALL = pl.CostEstimate(flops=1024, bytes_accessed=1024, transcendentals=0)


def eye():
    rows = lax.broadcasted_iota(jnp.int32, (BLOCK, BLOCK), 0)
    cols = lax.broadcasted_iota(jnp.int32, (BLOCK, BLOCK), 1)
    return rows == cols


def column_of(row):
    return jnp.sum(jnp.where(eye(), jnp.broadcast_to(row, (BLOCK, BLOCK)), 0.0), axis=1, keepdims=True)


def row_of(column):
    return jnp.sum(jnp.where(eye(), jnp.broadcast_to(column, (BLOCK, BLOCK)), 0.0), axis=0, keepdims=True)


def square_kernel(mixer_ref, gate_ref, out_ref):
    gate = gate_ref[...].astype(F32)
    gated = mixer_ref[...].astype(F32) * (gate * jax.nn.sigmoid(gate))
    out_ref[0] = row_of(jnp.sum(gated * gated, axis=1, keepdims=True))


def hidden_kernel(order_ref, mixer_ref, gate_ref, inverse_ref, gain_ref, out_ref, turned):
    gate = gate_ref[...].astype(F32)
    gated = mixer_ref[...].astype(F32) * (gate * jax.nn.sigmoid(gate))
    normed = gated * column_of(inverse_ref[0])
    hidden = normed * gain_ref[...]
    turned[...] = hidden.T
    x, zl = order_ref[16], order_ref[17]
    for k, (dx, dz) in enumerate(OWNERS):
        start = lax.rem(zl + dz, 2) * 256 + lax.rem(x + dx, N_X) * 64
        out_ref[k * 64 : (k + 1) * 64, :] = turned[pl.ds(pl.multiple_of(start, 64), 64), :].astype(BF16)


def centre_kernel(order_ref, back_ref, mixer_ref, gate_ref, inverse_ref, gain_ref, out_ref):
    gate = gate_ref[...].astype(F32)
    gated = mixer_ref[...].astype(F32) * (gate * jax.nn.sigmoid(gate))
    normed = gated * column_of(inverse_ref[0])
    scaled = back_ref[...] * gain_ref[...]
    out_ref[0] = row_of(jnp.sum(scaled * normed, axis=1, keepdims=True))


def grads_kernel(order_ref, back_ref, mixer_ref, gate_ref, inverse_ref, centre_ref, gain_ref, input_ref, gate_out_ref):
    gate = gate_ref[...].astype(F32)
    mixer = mixer_ref[...].astype(F32)
    sig = jax.nn.sigmoid(gate)
    activated = gate * sig
    slope = sig * (1.0 + gate * (1.0 - sig))
    inverse = column_of(inverse_ref[0])
    normed = mixer * activated * inverse
    scaled = back_ref[...] * gain_ref[...]
    gated_back = inverse * (scaled - normed * column_of(centre_ref[0]))
    input_ref[...] = (gated_back * activated).astype(BF16)
    gate_out_ref[...] = (gated_back * mixer * slope).astype(BF16)


def copies(sources, target, sems):
    start, made = 0, []
    for k, source in enumerate(sources):
        rows = source.shape[0]
        made.append(pltpu.make_async_copy(source, target.at[pl.ds(start, rows)], sems.at[k]))
        start += rows
    return made


def join_kernel(count, *refs):
    sources, out_ref, sems = refs[:count], refs[-2], refs[-1]
    made = copies(sources, out_ref, sems)
    for copy in made:
        copy.start()
    for copy in made:
        copy.wait()


def join(pieces, after, name):
    rows = sum(p.shape[0] for p in pieces)
    anywhere = pl.BlockSpec(memory_space=pl.ANY)
    return pl.pallas_call(
        lambda *refs: join_kernel(len(pieces), *refs),
        in_specs=[anywhere] * (len(pieces) + len(after)),
        out_specs=anywhere,
        out_shape=jax.ShapeDtypeStruct((rows, pieces[0].shape[1]), pieces[0].dtype),
        scratch_shapes=[pltpu.SemaphoreType.DMA((len(pieces),))],
        compiler_params=params(16),
        cost_estimate=SMALL,
        name=name,
    )(*pieces, *after)


def fetches(pieces, cot, sems, n):
    at, made = 0, []
    cols = pl.ds(n * TILE, TILE)
    for piece in pieces:
        rows = piece.shape[0]
        made.append(pltpu.make_async_copy(piece.at[:, cols], cot.at[pl.ds(at, rows), cols], sems.at[n, len(made)]))
        at += rows
    return made


def arrive(pieces, cot, sems, steps):
    n = pl.program_id(0)

    @pl.when(n == 0)
    def _():
        for k in range(steps):
            for copy in fetches(pieces, cot, sems, k):
                copy.start()

    for k in range(steps):

        @pl.when(n == k)
        def _():
            for copy in fetches(pieces, cot, sems, k):
                copy.wait()

    return cot[:, pl.ds(pl.multiple_of(n * TILE, TILE), TILE)]


def back_step(cot, weight_ref, sums, back_ref, start, sem, steps):
    n = pl.program_id(0)
    part = lax.dot_general(cot, weight_ref[...], (((1,), (1,)), ((), ())), preferred_element_type=F32)

    @pl.when(n == 0)
    def _():
        sums[...] = part

    @pl.when(n > 0)
    def _():
        sums[...] += part

    @pl.when(n == steps - 1)
    def _():
        out = pltpu.make_async_copy(sums, back_ref.at[pl.ds(start, sums.shape[0])], sem)
        out.start()
        out.wait()


def early_kernel(count, steps, *refs):
    pieces, (hidden_ref, weight_ref, grad_ref, back_ref, cot, sums, sems, sem) = refs[:count], refs[count:]
    here = arrive(pieces, cot, sems, steps)
    grad_ref[...] = jnp.dot(hidden_ref[...], here, preferred_element_type=F32)
    back_step(here, weight_ref, sums, back_ref, 0, sem, steps)


def late_kernel(count, steps, *refs):
    pieces, (hidden_ref, early_ref, *outs, mine_ref, cot, sems) = refs[:count], refs[count:]
    n = pl.program_id(0)
    here = arrive(pieces, cot, sems, steps)
    grad = early_ref[...] + jnp.dot(hidden_ref[...], here, preferred_element_type=F32)
    sent = len(outs)
    mine_ref[...] = grad[sent * 64 :]
    lanes = lax.broadcasted_iota(jnp.int32, (64, 128), 1)
    cols = pl.ds(pl.multiple_of(n * TILE, TILE), TILE)
    for k, out in enumerate(outs):
        rows = grad[k * 64 : (k + 1) * 64]
        most = jnp.maximum(jnp.max(jnp.abs(rows), axis=1, keepdims=True), 1e-30)
        code = jnp.ceil(jnp.log2(most) * FINE)
        out[:, cols] = jnp.round(rows * (TOP / scale_of(code))).astype(jnp.int32).astype(jnp.int16)
        codes = pl.ds(steps * TILE, 128)
        before = jnp.where(n == 0, 0, out[:, codes].astype(jnp.int32))
        out[:, codes] = jnp.where(lanes == n, code.astype(jnp.int32), before).astype(jnp.int16)


def scale_of(code):
    return jnp.exp(code * (0.6931471805599453 / FINE))


def back_kernel(count, start, steps, *refs):
    pieces, (weight_ref, back_in, back_ref, cot, sums, sems, sem) = refs[:count], refs[count:]
    here = arrive(pieces, cot, sems, steps)
    back_step(here, weight_ref, sums, back_ref, start, sem, steps)


def sum_kernel(count, *refs):
    codes, parts, (mine_ref, out_ref) = refs[:count], refs[count : 2 * count], refs[2 * count :]
    n = pl.program_id(0)
    lanes = lax.broadcasted_iota(jnp.int32, (64, 128), 1)
    total = mine_ref[...]
    for code_ref, part_ref in zip(codes, parts):
        code = jnp.where(lanes == n, code_ref[...].astype(jnp.int32).astype(F32), 0.0)
        scale = scale_of(jnp.sum(code, axis=1, keepdims=True)) / TOP
        total += part_ref[...].astype(jnp.int32).astype(F32) * scale
    out_ref[...] = total


ANYWHERE = pl.BlockSpec(memory_space=pl.ANY)


def wide(rows):
    return pl.BlockSpec((rows, TILE), lambda n: (0, n))


def kept(rows, cols, at=0):
    return pl.BlockSpec((rows, cols), lambda n: (0, at))


def early_products(pieces, hidden, weight):
    tokens = sum(p.shape[0] for p in pieces)
    channels, width = weight.shape
    steps = width // TILE
    return pl.pallas_call(
        lambda *refs: early_kernel(len(pieces), steps, *refs),
        grid=(steps,),
        in_specs=[ANYWHERE] * len(pieces) + [kept(channels, tokens), wide(channels)],
        out_specs=[wide(channels), ANYWHERE],
        out_shape=[jax.ShapeDtypeStruct((channels, width), F32), jax.ShapeDtypeStruct((2048, channels), F32)],
        scratch_shapes=[
            pltpu.VMEM((tokens, width), BF16),
            pltpu.VMEM((tokens, channels), F32),
            pltpu.SemaphoreType.DMA((steps, len(pieces))),
            pltpu.SemaphoreType.DMA,
        ],
        compiler_params=params(48),
        cost_estimate=SMALL,
        name="early_products",
    )(*pieces, hidden, weight)


def late_products(pieces, hidden, early):
    tokens = sum(p.shape[0] for p in pieces)
    channels, width = early.shape
    steps = width // TILE
    sent = len(OWNERS) - 1
    code = jax.ShapeDtypeStruct((64, width + 128), jnp.int16)
    return pl.pallas_call(
        lambda *refs: late_kernel(len(pieces), steps, *refs),
        grid=(steps,),
        in_specs=[ANYWHERE] * len(pieces) + [kept(channels, tokens), wide(channels)],
        out_specs=[kept(64, width + 128)] * sent + [wide(64)],
        out_shape=[code] * sent + [jax.ShapeDtypeStruct((64, width), F32)],
        scratch_shapes=[pltpu.VMEM((tokens, width), BF16), pltpu.SemaphoreType.DMA((steps, len(pieces)))],
        compiler_params=params(48),
        cost_estimate=SMALL,
        name="late_products",
    )(*pieces, hidden, early)


def late_back(pieces, weight, back, after):
    tokens = sum(p.shape[0] for p in pieces)
    channels, width = weight.shape
    steps = width // TILE
    start = back.shape[0] - tokens
    count = len(pieces)
    return pl.pallas_call(
        lambda *refs: back_kernel(count, start, steps, *refs[: count + 2], *refs[count + 3 :]),
        grid=(steps,),
        in_specs=[ANYWHERE] * count + [wide(channels), ANYWHERE, ANYWHERE],
        out_specs=ANYWHERE,
        out_shape=jax.ShapeDtypeStruct(back.shape, F32),
        input_output_aliases={count + 1: 0},
        scratch_shapes=[
            pltpu.VMEM((tokens, width), BF16),
            pltpu.VMEM((tokens, channels), F32),
            pltpu.SemaphoreType.DMA((steps, count)),
            pltpu.SemaphoreType.DMA,
        ],
        compiler_params=params(48),
        cost_estimate=SMALL,
        name="late_back",
    )(*pieces, weight, back, after)


def summed(codes, mine):
    width = mine.shape[1]
    return pl.pallas_call(
        lambda *refs: sum_kernel(len(codes), *refs),
        grid=(width // TILE,),
        in_specs=[kept(64, 128, width // 128)] * len(codes) + [wide(64)] * (len(codes) + 1),
        out_specs=wide(64),
        out_shape=jax.ShapeDtypeStruct(mine.shape, F32),
        compiler_params=params(32),
        cost_estimate=SMALL,
        name="summed",
    )(*codes, *codes, mine)


def adam_kernel(where_ref, grad_ref, up_ref, down_ref, master_ref, first_ref, second_ref, arrived_ref, *rest):
    new_master, new_first, new_second = rest[-3:]
    offset, moved, old_count, new_count = where_ref[1], where_ref[2], where_ref[3], where_ref[4]
    width = grad_ref.shape[1]
    slots = lax.broadcasted_iota(jnp.int32, (128, width), 0)
    pad = jnp.zeros((128 - CAP, width), F32)
    grads = jnp.concatenate([up_ref[...], grad_ref[...], down_ref[...], pad], axis=0)
    grad = pltpu.roll(grads, lax.rem(128 - offset, 128), 0)[:CAP] / 8.0

    def placed(k, ref):
        extra = jnp.concatenate([arrived_ref[k * HALO : (k + 1) * HALO, :], jnp.zeros((128 - HALO, width), F32)], axis=0)
        extra = pltpu.roll(extra, old_count, 0)
        joined = jnp.where(slots < old_count, jnp.concatenate([ref[0], pad], axis=0), extra)
        return pltpu.roll(joined, lax.rem(128 - moved, 128), 0)[:CAP]

    valid = slots[:CAP] < new_count
    first = beta_one * placed(1, first_ref) + (1.0 - beta_one) * grad
    new_first[0] = jnp.where(valid, first, 0.0)
    second = beta_two * placed(2, second_ref) + (1.0 - beta_two) * grad * grad
    new_second[0] = jnp.where(valid, second, 0.0)
    corr_one = 1.0 - beta_one**adam_step
    corr_two = 1.0 - beta_two**adam_step
    update = first / corr_one / (jnp.sqrt(second / corr_two) + adam_eps)
    master = placed(0, master_ref)
    new_master[0] = jnp.where(valid, master - learn_rate * (update + weight_decay * master), 0.0)


def adam(where, grad, up, down, states, arrived, made, start, width):
    tile = 512
    at = start // tile
    state_spec = pl.BlockSpec((1, CAP, tile), lambda i, w: (0, 0, at + i))
    part = lambda n: pl.BlockSpec((n, tile), lambda i, w: (0, i))
    whole = jax.ShapeDtypeStruct(states[0].shape, F32)
    in_specs = [part(64), part(HALO), part(HALO), state_spec, state_spec, state_spec]
    in_specs.append(pl.BlockSpec((3 * HALO, tile), lambda i, w: (0, at + i)))
    operands = [grad, up, down, *states, arrived]
    aliases = {}
    if made is not None:
        in_specs += [pl.BlockSpec(memory_space=pl.ANY)] * 3
        operands += made
        aliases = {8: 0, 9: 1, 10: 2}
    return pl.pallas_call(
        adam_kernel,
        grid_spec=pltpu.PrefetchScalarGridSpec(
            num_scalar_prefetch=1,
            grid=(width // tile,),
            in_specs=in_specs,
            out_specs=[state_spec] * 3,
        ),
        out_shape=[whole] * 3,
        input_output_aliases=aliases,
        compiler_params=params(32),
        cost_estimate=SMALL,
        name="adam",
    )(where, *operands)


def local(
    cotangent,
    mixer_out,
    gate,
    norm_gain,
    out_weight,
    old_master,
    old_first,
    old_second,
    old_bounds,
    new_bounds,
):
    dp = lax.axis_index("dp")
    tensor = lax.axis_index("tensor")
    x, zl = dp % 4, dp // 4
    y, zh, core = tensor // 4, (tensor // 2) % 2, tensor % 2
    tokens, channels = mixer_out.shape
    blocks = tokens // BLOCK

    old_row, new_row = old_bounds[0], new_bounds[0]
    new_start = new_row[dp]
    old_start = old_row[dp]
    where = jnp.stack(
        [x, new_start - (64 * dp - HALO), new_start - old_start, old_row[dp + 1] - old_start, new_row[dp + 1] - new_start]
    ).astype(jnp.int32)

    order = jnp.stack(
        [
            ((y + dy) % N_Y * 2 + (zh + dz) % 2) * 2 + (core + dc) % 2
            for group in (EARLY, LATE)
            for dc in (0, 1)
            for dy, dz in group
        ]
        + [x, zl]
    ).astype(jnp.int32)

    own = cotangent
    own_z = move(own, TO_ZHI)
    own_m, own_p = move(own, TO_YP), move(own, TO_YM)
    own_s = move(own, TO_CORE)

    row_spec = pl.BlockSpec((1, 1, BLOCK), lambda i: (i, 0, 0))
    block_spec = pl.BlockSpec((BLOCK, channels), lambda i: (i, 0))
    rows_shape = jax.ShapeDtypeStruct((blocks, 1, BLOCK), F32)

    def group_total(part):
        part = part + move(part, TO_CORE)
        return part + move(part, TO_ZHI)

    squares = pl.pallas_call(
        square_kernel,
        grid=(blocks,),
        in_specs=[block_spec, block_spec],
        out_specs=row_spec,
        out_shape=rows_shape,
        compiler_params=params(32),
        cost_estimate=SMALL,
        name="squares",
    )(mixer_out, gate)
    inverse = lax.rsqrt(group_total(squares) / GROUP + norm_eps)

    gain = norm_gain[None, :]
    there = pl.BlockSpec((BLOCK, channels), lambda i, o: (o[i], 0))
    here = pl.BlockSpec((BLOCK, channels), lambda i, o: (i, 0))
    there_row = pl.BlockSpec((1, 1, BLOCK), lambda i, o: (o[i], 0, 0))
    gain_spec = pl.BlockSpec((1, channels), lambda i, o: (0, 0))

    def ordered(kernel, in_specs, out_specs, out_shape, name, scratch=()):
        return pl.pallas_call(
            kernel,
            grid_spec=pltpu.PrefetchScalarGridSpec(
                num_scalar_prefetch=1, grid=(blocks,), in_specs=in_specs, out_specs=out_specs, scratch_shapes=scratch
            ),
            out_shape=out_shape,
            compiler_params=params(32),
            cost_estimate=SMALL,
            name=name,
        )

    hidden = ordered(
        hidden_kernel,
        [there, there, there_row, gain_spec],
        pl.BlockSpec((channels, BLOCK), lambda i, o: (0, i)),
        jax.ShapeDtypeStruct((channels, tokens), BF16),
        "hidden",
        [pltpu.VMEM((channels, BLOCK), F32)],
    )(order, mixer_out, gate, inverse, gain)

    states = (old_master, old_first, old_second)
    arrived = move(jnp.concatenate([s[0, :HALO] for s in states], axis=0), TO_LAST)

    far_a, far_b = move(own_m[:64], TO_YP), move(own_p[64:], TO_YM)
    other_m, other_p = move(own_z, TO_YP), move(own_z, TO_YM)
    near = move(join([own_z, own_m, own_p], [hidden], "near"), TO_CORE)
    far = join([far_a, far_b], [], "far")
    far_z, far_s = move(far, TO_ZHI), move(far, TO_CORE)
    early, back = early_products([own, own_z, own_m, own_p, far, own_s, near, far_s], hidden, out_weight)
    other = move(join([other_m, other_p, far_z], [early], "other"), TO_CORE)
    late = [other_m, other_p, far_z, other]
    *codes, mine = late_products(late, hidden[:, 1280:], early)
    back = late_back(late, out_weight, back, mine)
    grad = summed([move(code, pairs) for code, pairs in zip(codes, TO_OWNER)], mine)
    up = move(grad[64 - HALO :], TO_NEXT)
    down = move(grad[:HALO], TO_LAST)
    made = adam(where, grad, up, down, states, arrived, None, 0, grad.shape[1])

    centre = ordered(
        centre_kernel,
        [here, there, there, there_row, gain_spec],
        there_row,
        rows_shape,
        "centre",
    )(order, back, mixer_out, gate, inverse, gain)
    centre = group_total(centre) / GROUP
    out_shape = jax.ShapeDtypeStruct((tokens, channels), BF16)
    input_grad, gate_grad = ordered(
        grads_kernel,
        [here, there, there, there_row, there_row, gain_spec],
        [there, there],
        [out_shape, out_shape],
        "grads",
    )(order, back, mixer_out, gate, inverse, centre, gain)
    return (*made, input_grad, gate_grad)


def solution(mesh):
    return jax.shard_map(
        local,
        mesh=mesh,
        in_specs=(
            P(("dp", "tensor"), None),
            P("dp", "tensor"),
            P("dp", "tensor"),
            P("tensor"),
            P("tensor", None),
            P("tensor", "dp", None),
            P("tensor", "dp", None),
            P("tensor", "dp", None),
            P("tensor", None),
            P("tensor", None),
        ),
        out_specs=(
            P("tensor", "dp", None),
            P("tensor", "dp", None),
            P("tensor", "dp", None),
            P("dp", "tensor"),
            P("dp", "tensor"),
        ),
        check_vma=False,
    )
```

```python
import jax
import jax.numpy as jnp
from jax import lax
from jax.experimental import pallas as pl
from jax.experimental.pallas import tpu as pltpu
from jax.sharding import PartitionSpec as P

GROUP = 2048

norm_eps = 1e-05
beta_one = 0.9
beta_two = 0.95
adam_eps = 1e-08
learn_rate = 0.0003
weight_decay = 0.1
adam_step = 1000.0

N_X, N_Y = 4, 4
AXES = ("dp", "tensor")
TILE = 1024
TOP, FINE = 32700.0, 256.0
BLOCK = 128
HALO = 16
CAP = 96
OWNERS = ((1, 0), (1, 1), (3, 0), (3, 1), (2, 0), (2, 1), (0, 0), (0, 1))
HALF = 2048
GRANT = 24
EARLY = ((0, 0), (0, 1), (3, 0), (1, 0))
MIDDLE = ((2, 0), (1, 1), (3, 1))
LATE = ((2, 1),)
F32 = jnp.float32
BF16 = jnp.bfloat16


def position(flat):
    dp, tensor = flat // 16, flat % 16
    return dp % 4, tensor // 4, dp // 4, (tensor // 2) % 2, tensor % 2


def flat_of(x, y, zl, zh, c):
    return (zl * 4 + x) * 16 + (y * 2 + zh) * 2 + c


def pairs_of(move):
    return [(i, flat_of(*move(*position(i)))) for i in range(128)]


TO_CORE = pairs_of(lambda x, y, zl, zh, c: (x, y, zl, zh, 1 - c))
TO_ZHI = pairs_of(lambda x, y, zl, zh, c: (x, y, zl, 1 - zh, c))
TO_YP = pairs_of(lambda x, y, zl, zh, c: (x, (y + 1) % N_Y, zl, zh, c))
TO_YM = pairs_of(lambda x, y, zl, zh, c: (x, (y - 1) % N_Y, zl, zh, c))
TO_ZLO = pairs_of(lambda x, y, zl, zh, c: (x, y, 1 - zl, zh, c))
TO_X = [pairs_of(lambda x, y, zl, zh, c: ((x + dx) % N_X, y, zl, zh, c)) for dx in (1, 3, 2)]
TO_NEXT = [(i, i + 16) for i in range(112)]
TO_LAST = [(i + 16, i) for i in range(112)]


def move(value, pairs):
    return lax.ppermute(value, AXES, pairs)


def tied(value, other):
    late = other[(0,) * other.ndim] > 1e38
    return jnp.where(late, jnp.zeros_like(value), value)


def params(mib):
    return pltpu.CompilerParams(vmem_limit_bytes=mib * 2**20)


def cost(time):
    return pl.CostEstimate(flops=0, bytes_accessed=int(time * 3.3e6), transcendentals=0)


def eye():
    rows = lax.broadcasted_iota(jnp.int32, (BLOCK, BLOCK), 0)
    cols = lax.broadcasted_iota(jnp.int32, (BLOCK, BLOCK), 1)
    return rows == cols


def column_of(row):
    return jnp.sum(jnp.where(eye(), jnp.broadcast_to(row, (BLOCK, BLOCK)), 0.0), axis=1, keepdims=True)


def row_of(column):
    return jnp.sum(jnp.where(eye(), jnp.broadcast_to(column, (BLOCK, BLOCK)), 0.0), axis=0, keepdims=True)


def square_kernel(mixer_ref, gate_ref, out_ref):
    gate = gate_ref[...].astype(F32)
    gated = mixer_ref[...].astype(F32) * (gate * jax.nn.sigmoid(gate))
    total = jnp.sum(gated * gated, axis=1, keepdims=True)
    for k in range(out_ref.shape[0]):
        out_ref[k] = row_of(total[k * BLOCK : (k + 1) * BLOCK])


def hidden_kernel(order_ref, mixer_ref, gate_ref, inverse_ref, gain_ref, out_ref, turned):
    gate = gate_ref[...].astype(F32)
    gated = mixer_ref[...].astype(F32) * (gate * jax.nn.sigmoid(gate))
    normed = gated * column_of(inverse_ref[0])
    hidden = normed * gain_ref[...]
    turned[...] = hidden.T
    x, zl = order_ref[16], order_ref[17]
    for k, (dx, dz) in enumerate(OWNERS):
        start = lax.rem(zl + dz, 2) * 256 + lax.rem(x + dx, N_X) * 64
        out_ref[k * 64 : (k + 1) * 64, :] = turned[pl.ds(pl.multiple_of(start, 64), 64), :].astype(BF16)


def centre_kernel(order_ref, back_ref, mixer_ref, gate_ref, inverse_ref, gain_ref, out_ref):
    gate = gate_ref[...].astype(F32)
    gated = mixer_ref[...].astype(F32) * (gate * jax.nn.sigmoid(gate))
    normed = gated * column_of(inverse_ref[0])
    scaled = back_ref[...] * gain_ref[...]
    out_ref[0] = row_of(jnp.sum(scaled * normed, axis=1, keepdims=True))


def grads_kernel(order_ref, back_ref, mixer_ref, gate_ref, inverse_ref, centre_ref, gain_ref, input_ref, gate_out_ref):
    gate = gate_ref[...].astype(F32)
    mixer = mixer_ref[...].astype(F32)
    sig = jax.nn.sigmoid(gate)
    activated = gate * sig
    slope = sig * (1.0 + gate * (1.0 - sig))
    inverse = column_of(inverse_ref[0])
    normed = mixer * activated * inverse
    scaled = back_ref[...] * gain_ref[...]
    gated_back = inverse * (scaled - normed * column_of(centre_ref[0]))
    input_ref[...] = (gated_back * activated).astype(BF16)
    gate_out_ref[...] = (gated_back * mixer * slope).astype(BF16)


def fetches(pieces, cot, sems, n):
    at, made = 0, []
    cols = pl.ds(n * TILE, TILE)
    for piece in pieces:
        rows = piece.shape[0]
        made.append(pltpu.make_async_copy(piece.at[:, cols], cot.at[pl.ds(at, rows), cols], sems.at[n, len(made)]))
        at += rows
    return made


def arrive(pieces, cot, sems, steps, others=()):
    n = pl.program_id(0)

    @pl.when(n == 0)
    def _():
        for copy in others:
            copy.start()
        for k in range(steps):
            for copy in fetches(pieces, cot, sems, k):
                copy.start()
        for copy in others:
            copy.wait()

    for k in range(steps):

        @pl.when(n == k)
        def _():
            for copy in fetches(pieces, cot, sems, k):
                copy.wait()

    return cot[:, pl.ds(pl.multiple_of(n * TILE, TILE), TILE)]


def columns_of(hidden_ref, start, hid, sem):
    return pltpu.make_async_copy(hidden_ref.at[:, pl.ds(start, hid.shape[1])], hid, sem)


def back_step(cot, weight_ref, sums, back_ref, start, sem, steps):
    n = pl.program_id(0)
    part = lax.dot_general(cot, weight_ref[...], (((1,), (1,)), ((), ())), preferred_element_type=F32)

    @pl.when(n == 0)
    def _():
        sums[...] = part

    @pl.when(n > 0)
    def _():
        sums[...] += part

    @pl.when(n == steps - 1)
    def _():
        out = pltpu.make_async_copy(sums, back_ref.at[pl.ds(start, sums.shape[0])], sem)
        out.start()
        out.wait()


def first_kernel(count, start, steps, *refs):
    pieces, (hidden_ref, weight_ref, grad_ref, back_ref, cot, hid, sums, sems, sem) = refs[:count], refs[count:]
    here = arrive(pieces, cot, sems, steps, [columns_of(hidden_ref, start, hid, sem)])
    grad_ref[...] = jnp.dot(hid[...], here, preferred_element_type=F32)
    back_step(here, weight_ref, sums, back_ref, start, sem, steps)


def next_kernel(count, start, steps, *refs):
    pieces = refs[:count]
    hidden_ref, weight_ref, before_ref, _, grad_ref, back_ref, cot, hid, sums, sems, sem = refs[count:]
    here = arrive(pieces, cot, sems, steps, [columns_of(hidden_ref, start, hid, sem)])
    grad_ref[...] = before_ref[...] + jnp.dot(hid[...], here, preferred_element_type=F32)
    back_step(here, weight_ref, sums, back_ref, start, sem, steps)


def scale_of(code):
    return jnp.exp(code * (0.6931471805599453 / FINE))


def encode(rows, out, start, n):
    here = pl.ds(start, rows.shape[0])
    most = jnp.maximum(jnp.max(jnp.abs(rows), axis=1, keepdims=True), 1e-30)
    code = jnp.ceil(jnp.log2(most) * FINE)
    cols = pl.ds(pl.multiple_of(n * TILE, TILE), TILE)
    out[here, cols] = jnp.round(rows * (TOP / scale_of(code))).astype(jnp.int32).astype(jnp.int16)
    lanes = lax.broadcasted_iota(jnp.int32, (rows.shape[0], 128), 1)
    before = jnp.where(n == 0, 0, out[here, HALF:].astype(jnp.int32))
    out[here, HALF:] = jnp.where(lanes == n, code.astype(jnp.int32), before).astype(jnp.int16)


def decode(part_ref, code_ref, n):
    lanes = lax.broadcasted_iota(jnp.int32, code_ref.shape, 1)
    code = jnp.where(lanes == n, code_ref[...].astype(jnp.int32).astype(F32), 0.0)
    scale = scale_of(jnp.sum(code, axis=1, keepdims=True)) / TOP
    return part_ref[...].astype(jnp.int32).astype(F32) * scale


def late_kernel(count, start, steps, *refs):
    pieces = refs[:count]
    hidden_ref, weight_ref, before_ref, _, *to_x, to_z, mine_a, mine_b, back_ref, cot, hid, sums, sems, sem = refs[count:]
    n = pl.program_id(0)
    here = arrive(pieces, cot, sems, steps, [columns_of(hidden_ref, start, hid, sem)])
    back_step(here, weight_ref, sums, back_ref, start, sem, steps)
    grad = before_ref[...] + jnp.dot(hid[...], here, preferred_element_type=F32)

    @pl.when(n < steps // 2)
    def _():
        for k, out in enumerate(to_x):
            encode(grad[k * 128 : (k + 1) * 128], out, 0, n)
        mine_a[...] = grad[384:]

    @pl.when(n >= steps // 2)
    def _():
        for k in range(4):
            encode(grad[k * 128 + 64 : (k + 1) * 128], to_z, k * 64, n - steps // 2)
            mine_b[k * 64 : (k + 1) * 64] = grad[k * 128 : k * 128 + 64]


def middle_kernel(*refs):
    got_a, got_z, (mine_a, mine_b) = refs[:6], refs[6:8], refs[8:10]
    send_a, *send_b, keep_a, keep_b = refs[-6:]
    n = pl.program_id(0)
    total = mine_a[...]
    for k in range(3):
        total += decode(got_a[2 * k], got_a[2 * k + 1], n)
    keep_a[...] = total[:64]
    encode(total[64:], send_a, 0, n)
    total = mine_b[...] + decode(got_z[0], got_z[1], n)
    for k, out in enumerate(send_b):
        encode(total[k * 64 : (k + 1) * 64], out, 0, n)
    keep_b[...] = total[192:]


def sum_kernel(*refs):
    got_a, got_b, (keep_a, keep_b) = refs[:2], refs[2:8], refs[8:10]
    out_ref, up_ref, down_ref = refs[-3:]
    n = pl.program_id(0)
    total_a = keep_a[...] + decode(got_a[0], got_a[1], n)
    total_b = keep_b[...]
    for k in range(3):
        total_b += decode(got_b[2 * k], got_b[2 * k + 1], n)
    for total, start in ((total_a, 0), (total_b, HALF)):
        cols = pl.ds(pl.multiple_of(start + n * TILE, TILE), TILE)
        out_ref[:, cols] = total
        up_ref[:, cols] = total[64 - HALO :]
        down_ref[:, cols] = total[:HALO]


ANYWHERE = pl.BlockSpec(memory_space=pl.ANY)


def wide(rows):
    return pl.BlockSpec((rows, TILE), lambda n: (0, n))


def kept(rows, cols, at=0):
    return pl.BlockSpec((rows, cols), lambda n: (0, at))


def products(pieces, hidden, weight, start, before=None):
    tokens = sum(p.shape[0] for p in pieces)
    channels, width = weight.shape
    steps, count = width // TILE, len(pieces)
    grad = jax.ShapeDtypeStruct((channels, width), F32)
    back = jax.ShapeDtypeStruct((hidden.shape[1], channels), F32)
    kernel = first_kernel if before is None else next_kernel
    return pl.pallas_call(
        lambda *refs: kernel(count, start, steps, *refs),
        grid=(steps,),
        in_specs=[ANYWHERE] * (count + 1) + [wide(channels)] + ([] if before is None else [wide(channels), ANYWHERE]),
        out_specs=[wide(channels), ANYWHERE],
        out_shape=[grad, back],
        input_output_aliases={} if before is None else {count + 3: 1},
        scratch_shapes=[
            pltpu.VMEM((tokens, width), BF16),
            pltpu.VMEM((channels, tokens), BF16),
            pltpu.VMEM((tokens, channels), F32),
            pltpu.SemaphoreType.DMA((steps, count)),
            pltpu.SemaphoreType.DMA,
        ],
        compiler_params=params(GRANT),
        cost_estimate=cost(18 if before is None else 16),
        name="products",
    )(*pieces, hidden, weight, *(before or []))


def late_products(pieces, hidden, weight, start, before):
    tokens = sum(p.shape[0] for p in pieces)
    channels, width = weight.shape
    steps, count = width // TILE, len(pieces)
    half = steps // 2
    code = lambda rows: jax.ShapeDtypeStruct((rows, HALF + 128), jnp.int16)
    full = lambda rows: jax.ShapeDtypeStruct((rows, HALF), F32)
    back = jax.ShapeDtypeStruct(before[1].shape, F32)
    return pl.pallas_call(
        lambda *refs: late_kernel(count, start, steps, *refs),
        grid=(steps,),
        in_specs=[ANYWHERE] * (count + 1) + [wide(channels), wide(channels), ANYWHERE],
        out_specs=[kept(128, HALF + 128)] * 3
        + [
            kept(256, HALF + 128),
            pl.BlockSpec((128, TILE), lambda n: (0, jnp.minimum(n, half - 1))),
            pl.BlockSpec((256, TILE), lambda n: (0, jnp.maximum(n - half, 0))),
            ANYWHERE,
        ],
        out_shape=[code(128)] * 3 + [code(256), full(128), full(256), back],
        input_output_aliases={count + 3: 6},
        scratch_shapes=[
            pltpu.VMEM((tokens, width), BF16),
            pltpu.VMEM((channels, tokens), BF16),
            pltpu.VMEM((tokens, channels), F32),
            pltpu.SemaphoreType.DMA((steps, count)),
            pltpu.SemaphoreType.DMA,
        ],
        compiler_params=params(GRANT),
        cost_estimate=cost(9),
        name="late_products",
    )(*pieces, hidden, weight, *before)


def coded(rows):
    return [wide(rows), kept(rows, 128, HALF // 128)]


def twice(arrays):
    return [a for array in arrays for a in (array, array)]


def middle_sums(got_a, got_z, mine_a, mine_b, after):
    code = jax.ShapeDtypeStruct((64, HALF + 128), jnp.int16)
    keep = jax.ShapeDtypeStruct((64, HALF), F32)
    return pl.pallas_call(
        middle_kernel,
        grid=(HALF // TILE,),
        in_specs=coded(128) * 3 + coded(256) + [wide(128), wide(256)] + [ANYWHERE] * len(after),
        out_specs=[kept(64, HALF + 128)] * 4 + [wide(64)] * 2,
        out_shape=[code] * 4 + [keep] * 2,
        compiler_params=params(GRANT),
        cost_estimate=cost(3),
        name="middle_sums",
    )(*twice(got_a), *twice([got_z]), mine_a, mine_b, *after)


def last_sums(got_a, got_b, keep_a, keep_b, after):
    width = 2 * HALF
    return pl.pallas_call(
        sum_kernel,
        grid=(HALF // TILE,),
        in_specs=coded(64) * 4 + [wide(64)] * 2 + [ANYWHERE] * len(after),
        out_specs=[kept(64, width), kept(HALO, width), kept(HALO, width)],
        out_shape=[jax.ShapeDtypeStruct((rows, width), F32) for rows in (64, HALO, HALO)],
        compiler_params=params(GRANT),
        cost_estimate=cost(3),
        name="last_sums",
    )(*twice([got_a]), *twice(got_b), keep_a, keep_b, *after)


def bounds_of(order_ref, old_ref, new_ref):
    dp = order_ref[17] * 4 + order_ref[16]
    new_start, old_start = new_ref[0, dp], old_ref[0, dp]
    return new_start - (64 * dp - HALO), new_start - old_start, old_ref[0, dp + 1] - old_start, new_ref[0, dp + 1] - new_start


def back_by(rows, by):
    return pltpu.roll(rows, lax.rem(128 - by, 128), 0)[:CAP]


def place_kernel(order_ref, old_ref, new_ref, *refs):
    states, arrived_ref, outs = refs[:3], refs[3], refs[4:]
    _, moved, old_count, _ = bounds_of(order_ref, old_ref, new_ref)
    width = arrived_ref.shape[1]
    slots = lax.broadcasted_iota(jnp.int32, (128, width), 0)
    pad = jnp.zeros((128 - CAP, width), F32)
    for k, (ref, out) in enumerate(zip(states, outs)):
        extra = jnp.concatenate([arrived_ref[k * HALO : (k + 1) * HALO, :], jnp.zeros((128 - HALO, width), F32)], axis=0)
        extra = pltpu.roll(extra, old_count, 0)
        out[...] = back_by(jnp.where(slots < old_count, jnp.concatenate([ref[0], pad], axis=0), extra), moved)


def adam_kernel(order_ref, old_ref, new_ref, grad_ref, up_ref, down_ref, master_ref, first_ref, second_ref, *outs):
    new_master, new_first, new_second = outs
    offset, _, _, new_count = bounds_of(order_ref, old_ref, new_ref)
    width = grad_ref.shape[1]
    pad = jnp.zeros((128 - CAP, width), F32)
    grad = back_by(jnp.concatenate([up_ref[...], grad_ref[...], down_ref[...], pad], axis=0), offset) / 8.0
    valid = lax.broadcasted_iota(jnp.int32, (CAP, width), 0) < new_count
    first = beta_one * first_ref[...] + (1.0 - beta_one) * grad
    new_first[0] = jnp.where(valid, first, 0.0)
    second = beta_two * second_ref[...] + (1.0 - beta_two) * grad * grad
    new_second[0] = jnp.where(valid, second, 0.0)
    corr_one = 1.0 - beta_one**adam_step
    corr_two = 1.0 - beta_two**adam_step
    update = first / corr_one / (jnp.sqrt(second / corr_two) + adam_eps)
    master = master_ref[...]
    new_master[0] = jnp.where(valid, master - learn_rate * (update + weight_decay * master), 0.0)


def share_call(kernel, tile, in_specs, out_specs, out_shape, name):
    width = 2 * HALF
    return pl.pallas_call(
        kernel,
        grid_spec=pltpu.PrefetchScalarGridSpec(
            num_scalar_prefetch=3, grid=(width // tile,), in_specs=in_specs, out_specs=out_specs
        ),
        out_shape=out_shape,
        compiler_params=params(GRANT),
        cost_estimate=cost(6),
        name=name,
    )


def place(scalars, states, arrived):
    tile = 1024
    state = pl.BlockSpec((1, CAP, tile), lambda i, *_: (0, 0, i))
    part = lambda n: pl.BlockSpec((n, tile), lambda i, *_: (0, i))
    out = jax.ShapeDtypeStruct(states[0].shape[1:], F32)
    return share_call(place_kernel, tile, [state] * 3 + [part(3 * HALO)], [part(CAP)] * 3, [out] * 3, "place")(
        *scalars, *states, arrived
    )


def adam(scalars, grad, up, down, placed):
    tile = 1024
    state = pl.BlockSpec((1, CAP, tile), lambda i, *_: (0, 0, i))
    part = lambda n: pl.BlockSpec((n, tile), lambda i, *_: (0, i))
    out = jax.ShapeDtypeStruct((1, *placed[0].shape), F32)
    in_specs = [part(64), part(HALO), part(HALO)] + [part(CAP)] * 3
    return share_call(adam_kernel, tile, in_specs, [state] * 3, [out] * 3, "adam")(*scalars, grad, up, down, *placed)


def local(
    cotangent,
    mixer_out,
    gate,
    norm_gain,
    out_weight,
    old_master,
    old_first,
    old_second,
    old_bounds,
    new_bounds,
):
    dp = lax.axis_index("dp")
    tensor = lax.axis_index("tensor")
    x, zl = dp % 4, dp // 4
    y, zh, core = tensor // 4, (tensor // 2) % 2, tensor % 2
    tokens, channels = mixer_out.shape
    blocks = tokens // BLOCK

    order = jnp.stack(
        [
            ((y + dy) % N_Y * 2 + (zh + dz) % 2) * 2 + (core + dc) % 2
            for group in (EARLY, MIDDLE, LATE)
            for dc in (0, 1)
            for dy, dz in group
        ]
        + [x, zl]
    ).astype(jnp.int32)

    row_spec = pl.BlockSpec((4, 1, BLOCK), lambda i: (i, 0, 0))
    block_spec = pl.BlockSpec((4 * BLOCK, channels), lambda i: (i, 0))
    rows_shape = jax.ShapeDtypeStruct((blocks, 1, BLOCK), F32)

    def chip_total(part):
        return part + move(part, TO_CORE)

    def group_total(part):
        return part + move(part, TO_ZHI)

    squares = pl.pallas_call(
        square_kernel,
        grid=(blocks // 4,),
        in_specs=[block_spec, block_spec],
        out_specs=row_spec,
        out_shape=rows_shape,
        compiler_params=params(60),
        cost_estimate=cost(3),
        name="squares",
    )(mixer_out, gate)
    squares = chip_total(squares)
    inverse = lax.rsqrt(group_total(squares) / GROUP + norm_eps)

    gain = norm_gain[None, :]
    there = pl.BlockSpec((BLOCK, channels), lambda i, o: (o[i], 0))
    here = pl.BlockSpec((BLOCK, channels), lambda i, o: (i, 0))
    there_row = pl.BlockSpec((1, 1, BLOCK), lambda i, o: (o[i], 0, 0))
    gain_spec = pl.BlockSpec((1, channels), lambda i, o: (0, 0))

    def ordered(kernel, in_specs, out_specs, out_shape, name, time, scratch=()):
        return pl.pallas_call(
            kernel,
            grid_spec=pltpu.PrefetchScalarGridSpec(
                num_scalar_prefetch=1, grid=(blocks,), in_specs=in_specs, out_specs=out_specs, scratch_shapes=scratch
            ),
            out_shape=out_shape,
            compiler_params=params(16),
            cost_estimate=cost(time),
            name=name,
        )

    hidden = ordered(
        hidden_kernel,
        [there, there, there_row, gain_spec],
        pl.BlockSpec((channels, BLOCK), lambda i, o: (0, i)),
        jax.ShapeDtypeStruct((channels, tokens), BF16),
        "hidden",
        5,
        [pltpu.VMEM((channels, BLOCK), F32)],
    )(order, mixer_out, gate, inverse, gain)

    states = (old_master, old_first, old_second)
    arrived = move(jnp.concatenate([s[0, :HALO] for s in states], axis=0), TO_LAST)

    own = cotangent
    own_z = move(own, TO_ZHI)
    own_m, own_p = move(own, TO_YP), move(own, TO_YM)
    own_s = move(own, TO_CORE)
    own_z, own_m = tied(own_z, squares), tied(own_m, squares)
    far = move(own_m, TO_YP)
    other_p, other_m = move(own_z, TO_YM), move(own_m, TO_ZHI)
    early = [own, own_z, own_m, own_p, own_s, move(own_z, TO_CORE), move(own_m, TO_CORE), move(own_p, TO_CORE)]
    at = 0
    sums = products(early, hidden, out_weight, at)
    at += 8 * BLOCK
    half = BLOCK // 2
    last_a = move(tied(other_m[:half], sums[0]), TO_YP)
    last_b = move(tied(other_p[half:], sums[0]), TO_YM)
    middle = [far, other_p, other_m, move(far, TO_CORE), move(other_p, TO_CORE), move(other_m, TO_CORE)]
    sums = products(middle, hidden, out_weight, at, sums)
    at += 6 * BLOCK
    last_a, last_b = tied(last_a, sums[0]), tied(last_b, sums[0])
    last = [last_a, last_b, move(last_a, TO_CORE), move(last_b, TO_CORE)]
    *to_x, to_z, mine_a, mine_b, back = late_products(last, hidden, out_weight, at, sums)
    got_x, got_z = [move(code, pairs) for code, pairs in zip(to_x, TO_X)], move(to_z, TO_ZLO)

    centre = ordered(
        centre_kernel,
        [here, there, there, there_row, gain_spec],
        there_row,
        rows_shape,
        "centre",
        4,
    )(order, back, mixer_out, gate, inverse, gain)
    send_a, *send_b, keep_a, keep_b = middle_sums(got_x, got_z, mine_a, mine_b, [centre])
    centre = group_total(chip_total(centre)) / GROUP
    out_shape = jax.ShapeDtypeStruct((tokens, channels), BF16)
    input_grad, gate_grad = ordered(
        grads_kernel,
        [here, there, there, there_row, there_row, gain_spec],
        [there, there],
        [out_shape, out_shape],
        "grads",
        8,
    )(order, back, mixer_out, gate, inverse, centre, gain)

    scalars = (order, old_bounds, new_bounds)
    placed = place(scalars, states, arrived)
    got_a, got_b = move(send_a, TO_ZLO), [move(code, pairs) for code, pairs in zip(send_b, TO_X)]
    grad, last_rows, first_rows = last_sums(got_a, got_b, keep_a, keep_b, [input_grad, placed[0]])
    made = adam(scalars, grad, move(last_rows, TO_NEXT), move(first_rows, TO_LAST), placed)
    return (*made, input_grad, gate_grad)


def solution(mesh):
    return jax.shard_map(
        local,
        mesh=mesh,
        in_specs=(
            P(("dp", "tensor"), None),
            P("dp", "tensor"),
            P("dp", "tensor"),
            P("tensor"),
            P("tensor", None),
            P("tensor", "dp", None),
            P("tensor", "dp", None),
            P("tensor", "dp", None),
            P("tensor", None),
            P("tensor", None),
        ),
        out_specs=(
            P("tensor", "dp", None),
            P("tensor", "dp", None),
            P("tensor", "dp", None),
            P("dp", "tensor"),
            P("dp", "tensor"),
        ),
        check_vma=False,
    )
```

```python
import jax
import jax.numpy as jnp
from jax import lax
from jax.experimental import pallas as pl
from jax.experimental.pallas import tpu as pltpu
from jax.sharding import PartitionSpec as P

GROUP = 2048

norm_eps = 1e-05
beta_one = 0.9
beta_two = 0.95
adam_eps = 1e-08
learn_rate = 0.0003
weight_decay = 0.1
adam_step = 1000.0

N_X, N_Y = 4, 4
AXES = ("dp", "tensor")
TILE = 1024
TOP, FINE = 32700.0, 256.0
BLOCK = 128
HALO = 16
CAP = 96
OWNERS = ((1, 0), (1, 1), (3, 0), (3, 1), (2, 0), (2, 1), (0, 0), (0, 1))
HALF = 2048
GRANT = 24
EARLY = ((0, 0), (0, 1), (3, 0), (1, 0))
MIDDLE = ((2, 0), (1, 1), (3, 1))
LATE = ((2, 1),)
F32 = jnp.float32
BF16 = jnp.bfloat16


def position(flat):
    dp, tensor = flat // 16, flat % 16
    return dp % 4, tensor // 4, dp // 4, (tensor // 2) % 2, tensor % 2


def flat_of(x, y, zl, zh, c):
    return (zl * 4 + x) * 16 + (y * 2 + zh) * 2 + c


def pairs_of(move):
    return [(i, flat_of(*move(*position(i)))) for i in range(128)]


TO_CORE = pairs_of(lambda x, y, zl, zh, c: (x, y, zl, zh, 1 - c))
TO_ZHI = pairs_of(lambda x, y, zl, zh, c: (x, y, zl, 1 - zh, c))
TO_YP = pairs_of(lambda x, y, zl, zh, c: (x, (y + 1) % N_Y, zl, zh, c))
TO_YM = pairs_of(lambda x, y, zl, zh, c: (x, (y - 1) % N_Y, zl, zh, c))
TO_ZLO = pairs_of(lambda x, y, zl, zh, c: (x, y, 1 - zl, zh, c))
TO_X = [pairs_of(lambda x, y, zl, zh, c: ((x + dx) % N_X, y, zl, zh, c)) for dx in (1, 3, 2)]
TO_NEXT = [(i, i + 16) for i in range(112)]
TO_LAST = [(i + 16, i) for i in range(112)]


def move(value, pairs):
    return lax.ppermute(value, AXES, pairs)


def tied(value, other):
    late = other[(0,) * other.ndim] > 1e38
    return jnp.where(late, jnp.zeros_like(value), value)


def params(mib):
    return pltpu.CompilerParams(vmem_limit_bytes=mib * 2**20)


def cost(time):
    return pl.CostEstimate(flops=0, bytes_accessed=int(time * 3.3e6), transcendentals=0)


def eye():
    rows = lax.broadcasted_iota(jnp.int32, (BLOCK, BLOCK), 0)
    cols = lax.broadcasted_iota(jnp.int32, (BLOCK, BLOCK), 1)
    return rows == cols


def column_of(row):
    return jnp.sum(jnp.where(eye(), jnp.broadcast_to(row, (BLOCK, BLOCK)), 0.0), axis=1, keepdims=True)


def row_of(column):
    return jnp.sum(jnp.where(eye(), jnp.broadcast_to(column, (BLOCK, BLOCK)), 0.0), axis=0, keepdims=True)


def square_kernel(mixer_ref, gate_ref, out_ref):
    gate = gate_ref[...].astype(F32)
    gated = mixer_ref[...].astype(F32) * (gate * jax.nn.sigmoid(gate))
    total = jnp.sum(gated * gated, axis=1, keepdims=True)
    for k in range(out_ref.shape[0]):
        out_ref[k] = row_of(total[k * BLOCK : (k + 1) * BLOCK])


def hidden_kernel(order_ref, mixer_ref, gate_ref, inverse_ref, gain_ref, out_ref, turned):
    gate = gate_ref[...].astype(F32)
    gated = mixer_ref[...].astype(F32) * (gate * jax.nn.sigmoid(gate))
    normed = gated * column_of(inverse_ref[0])
    hidden = normed * gain_ref[...]
    turned[...] = hidden.T
    x, zl = order_ref[16], order_ref[17]
    for k, (dx, dz) in enumerate(OWNERS):
        start = lax.rem(zl + dz, 2) * 256 + lax.rem(x + dx, N_X) * 64
        out_ref[k * 64 : (k + 1) * 64, :] = turned[pl.ds(pl.multiple_of(start, 64), 64), :].astype(BF16)


def centre_kernel(order_ref, back_ref, mixer_ref, gate_ref, inverse_ref, gain_ref, out_ref):
    gate = gate_ref[...].astype(F32)
    gated = mixer_ref[...].astype(F32) * (gate * jax.nn.sigmoid(gate))
    normed = gated * column_of(inverse_ref[0])
    scaled = back_ref[...] * gain_ref[...]
    out_ref[0] = row_of(jnp.sum(scaled * normed, axis=1, keepdims=True))


def grads_kernel(order_ref, back_ref, mixer_ref, gate_ref, inverse_ref, centre_ref, gain_ref, input_ref, gate_out_ref):
    gate = gate_ref[...].astype(F32)
    mixer = mixer_ref[...].astype(F32)
    sig = jax.nn.sigmoid(gate)
    activated = gate * sig
    slope = sig * (1.0 + gate * (1.0 - sig))
    inverse = column_of(inverse_ref[0])
    normed = mixer * activated * inverse
    scaled = back_ref[...] * gain_ref[...]
    gated_back = inverse * (scaled - normed * column_of(centre_ref[0]))
    input_ref[...] = (gated_back * activated).astype(BF16)
    gate_out_ref[...] = (gated_back * mixer * slope).astype(BF16)


def fetches(pieces, cot, sems, n):
    at, made = 0, []
    cols = pl.ds(n * TILE, TILE)
    for piece in pieces:
        rows = piece.shape[0]
        made.append(pltpu.make_async_copy(piece.at[:, cols], cot.at[pl.ds(at, rows), cols], sems.at[n, len(made)]))
        at += rows
    return made


def arrive(pieces, cot, sems, steps, others=()):
    n = pl.program_id(0)

    @pl.when(n == 0)
    def _():
        for copy in others:
            copy.start()
        for k in range(steps):
            for copy in fetches(pieces, cot, sems, k):
                copy.start()
        for copy in others:
            copy.wait()

    for k in range(steps):

        @pl.when(n == k)
        def _():
            for copy in fetches(pieces, cot, sems, k):
                copy.wait()

    return cot[:, pl.ds(pl.multiple_of(n * TILE, TILE), TILE)]


def columns_of(hidden_ref, start, hid, sem):
    return pltpu.make_async_copy(hidden_ref.at[:, pl.ds(start, hid.shape[1])], hid, sem)


def back_step(cot, weight_ref, sums, back_ref, start, sem, steps):
    n = pl.program_id(0)
    part = lax.dot_general(cot, weight_ref[...], (((1,), (1,)), ((), ())), preferred_element_type=F32)

    @pl.when(n == 0)
    def _():
        sums[...] = part

    @pl.when(n > 0)
    def _():
        sums[...] += part

    @pl.when(n == steps - 1)
    def _():
        out = pltpu.make_async_copy(sums, back_ref.at[pl.ds(start, sums.shape[0])], sem)
        out.start()
        out.wait()


def first_kernel(count, start, steps, *refs):
    pieces, (hidden_ref, weight_ref, grad_ref, back_ref, cot, hid, sums, sems, sem) = refs[:count], refs[count:]
    here = arrive(pieces, cot, sems, steps, [columns_of(hidden_ref, start, hid, sem)])
    grad_ref[...] = jnp.dot(hid[...], here, preferred_element_type=F32)
    back_step(here, weight_ref, sums, back_ref, start, sem, steps)


def next_kernel(count, start, steps, *refs):
    pieces = refs[:count]
    hidden_ref, weight_ref, before_ref, _, grad_ref, back_ref, cot, hid, sums, sems, sem = refs[count:]
    here = arrive(pieces, cot, sems, steps, [columns_of(hidden_ref, start, hid, sem)])
    grad_ref[...] = before_ref[...] + jnp.dot(hid[...], here, preferred_element_type=F32)
    back_step(here, weight_ref, sums, back_ref, start, sem, steps)


def scale_of(code):
    return jnp.exp(code * (0.6931471805599453 / FINE))


def encode(rows, out, start, n):
    here = pl.ds(start, rows.shape[0])
    most = jnp.maximum(jnp.max(jnp.abs(rows), axis=1, keepdims=True), 1e-30)
    code = jnp.ceil(jnp.log2(most) * FINE)
    cols = pl.ds(pl.multiple_of(n * TILE, TILE), TILE)
    out[here, cols] = jnp.round(rows * (TOP / scale_of(code))).astype(jnp.int32).astype(jnp.int16)
    lanes = lax.broadcasted_iota(jnp.int32, (rows.shape[0], 128), 1)
    before = jnp.where(n == 0, 0, out[here, HALF:].astype(jnp.int32))
    out[here, HALF:] = jnp.where(lanes == n, code.astype(jnp.int32), before).astype(jnp.int16)


def decode(part_ref, code_ref, n):
    lanes = lax.broadcasted_iota(jnp.int32, code_ref.shape, 1)
    code = jnp.where(lanes == n, code_ref[...].astype(jnp.int32).astype(F32), 0.0)
    scale = scale_of(jnp.sum(code, axis=1, keepdims=True)) / TOP
    return part_ref[...].astype(jnp.int32).astype(F32) * scale


def late_kernel(count, start, steps, *refs):
    pieces = refs[:count]
    hidden_ref, weight_ref, before_ref, _, *to_x, to_z, mine_a, mine_b, back_ref, cot, hid, sums, sems, sem = refs[count:]
    n = pl.program_id(0)
    here = arrive(pieces, cot, sems, steps, [columns_of(hidden_ref, start, hid, sem)])
    back_step(here, weight_ref, sums, back_ref, start, sem, steps)
    grad = before_ref[...] + jnp.dot(hid[...], here, preferred_element_type=F32)

    @pl.when(n < steps // 2)
    def _():
        for k, out in enumerate(to_x):
            encode(grad[k * 128 : (k + 1) * 128], out, 0, n)
        mine_a[...] = grad[384:]

    @pl.when(n >= steps // 2)
    def _():
        for k in range(4):
            encode(grad[k * 128 + 64 : (k + 1) * 128], to_z, k * 64, n - steps // 2)
            mine_b[k * 64 : (k + 1) * 64] = grad[k * 128 : k * 128 + 64]


def middle_kernel(*refs):
    got_a, got_z, (mine_a, mine_b) = refs[:6], refs[6:8], refs[8:10]
    send_a, *send_b, keep_a, keep_b = refs[-6:]
    n = pl.program_id(0)
    total = mine_a[...]
    for k in range(3):
        total += decode(got_a[2 * k], got_a[2 * k + 1], n)
    keep_a[...] = total[:64]
    encode(total[64:], send_a, 0, n)
    total = mine_b[...] + decode(got_z[0], got_z[1], n)
    for k, out in enumerate(send_b):
        encode(total[k * 64 : (k + 1) * 64], out, 0, n)
    keep_b[...] = total[192:]


def sum_kernel(*refs):
    got_a, got_b, (keep_a, keep_b) = refs[:2], refs[2:8], refs[8:10]
    out_ref, up_ref, down_ref = refs[-3:]
    n = pl.program_id(0)
    total_a = keep_a[...] + decode(got_a[0], got_a[1], n)
    total_b = keep_b[...]
    for k in range(3):
        total_b += decode(got_b[2 * k], got_b[2 * k + 1], n)
    for total, start in ((total_a, 0), (total_b, HALF)):
        cols = pl.ds(pl.multiple_of(start + n * TILE, TILE), TILE)
        out_ref[:, cols] = total
        up_ref[:, cols] = total[64 - HALO :]
        down_ref[:, cols] = total[:HALO]


ANYWHERE = pl.BlockSpec(memory_space=pl.ANY)


def wide(rows):
    return pl.BlockSpec((rows, TILE), lambda n: (0, n))


def kept(rows, cols, at=0):
    return pl.BlockSpec((rows, cols), lambda n: (0, at))


def products(pieces, hidden, weight, start, before=None):
    tokens = sum(p.shape[0] for p in pieces)
    channels, width = weight.shape
    steps, count = width // TILE, len(pieces)
    grad = jax.ShapeDtypeStruct((channels, width), F32)
    back = jax.ShapeDtypeStruct((hidden.shape[1], channels), F32)
    kernel = first_kernel if before is None else next_kernel
    return pl.pallas_call(
        lambda *refs: kernel(count, start, steps, *refs),
        grid=(steps,),
        in_specs=[ANYWHERE] * (count + 1) + [wide(channels)] + ([] if before is None else [wide(channels), ANYWHERE]),
        out_specs=[wide(channels), ANYWHERE],
        out_shape=[grad, back],
        input_output_aliases={} if before is None else {count + 3: 1},
        scratch_shapes=[
            pltpu.VMEM((tokens, width), BF16),
            pltpu.VMEM((channels, tokens), BF16),
            pltpu.VMEM((tokens, channels), F32),
            pltpu.SemaphoreType.DMA((steps, count)),
            pltpu.SemaphoreType.DMA,
        ],
        compiler_params=params(GRANT),
        cost_estimate=cost(18 if before is None else 16),
        name="products",
    )(*pieces, hidden, weight, *(before or []))


def late_products(pieces, hidden, weight, start, before, arrived):
    tokens = sum(p.shape[0] for p in pieces)
    channels, width = weight.shape
    steps, count = width // TILE, len(pieces)
    half = steps // 2
    code = lambda rows: jax.ShapeDtypeStruct((rows, HALF + 128), jnp.int16)
    full = lambda rows: jax.ShapeDtypeStruct((rows, HALF), F32)
    back = jax.ShapeDtypeStruct(before[1].shape, F32)
    return pl.pallas_call(
        lambda *refs: late_kernel(count, start, steps, *refs[: count + 4], *refs[count + 5 :]),
        grid=(steps,),
        in_specs=[ANYWHERE] * (count + 1) + [wide(channels), wide(channels), ANYWHERE, ANYWHERE],
        out_specs=[kept(128, HALF + 128)] * 3
        + [
            kept(256, HALF + 128),
            pl.BlockSpec((128, TILE), lambda n: (0, jnp.minimum(n, half - 1))),
            pl.BlockSpec((256, TILE), lambda n: (0, jnp.maximum(n - half, 0))),
            ANYWHERE,
        ],
        out_shape=[code(128)] * 3 + [code(256), full(128), full(256), back],
        input_output_aliases={count + 3: 6},
        scratch_shapes=[
            pltpu.VMEM((tokens, width), BF16),
            pltpu.VMEM((channels, tokens), BF16),
            pltpu.VMEM((tokens, channels), F32),
            pltpu.SemaphoreType.DMA((steps, count)),
            pltpu.SemaphoreType.DMA,
        ],
        compiler_params=params(GRANT),
        cost_estimate=cost(9),
        name="late_products",
    )(*pieces, hidden, weight, *before, arrived)


def coded(rows):
    return [wide(rows), kept(rows, 128, HALF // 128)]


def twice(arrays):
    return [a for array in arrays for a in (array, array)]


def middle_sums(got_a, got_z, mine_a, mine_b, after):
    code = jax.ShapeDtypeStruct((64, HALF + 128), jnp.int16)
    keep = jax.ShapeDtypeStruct((64, HALF), F32)
    return pl.pallas_call(
        middle_kernel,
        grid=(HALF // TILE,),
        in_specs=coded(128) * 3 + coded(256) + [wide(128), wide(256)] + [ANYWHERE] * len(after),
        out_specs=[kept(64, HALF + 128)] * 4 + [wide(64)] * 2,
        out_shape=[code] * 4 + [keep] * 2,
        compiler_params=params(GRANT),
        cost_estimate=cost(3),
        name="middle_sums",
    )(*twice(got_a), *twice([got_z]), mine_a, mine_b, *after)


def last_sums(got_a, got_b, keep_a, keep_b, after):
    width = 2 * HALF
    return pl.pallas_call(
        sum_kernel,
        grid=(HALF // TILE,),
        in_specs=coded(64) * 4 + [wide(64)] * 2 + [ANYWHERE] * len(after),
        out_specs=[kept(64, width), kept(HALO, width), kept(HALO, width)],
        out_shape=[jax.ShapeDtypeStruct((rows, width), F32) for rows in (64, HALO, HALO)],
        compiler_params=params(GRANT),
        cost_estimate=cost(3),
        name="last_sums",
    )(*twice([got_a]), *twice(got_b), keep_a, keep_b, *after)


def bounds_of(order_ref, old_ref, new_ref):
    dp = order_ref[17] * 4 + order_ref[16]
    new_start, old_start = new_ref[0, dp], old_ref[0, dp]
    return new_start - (64 * dp - HALO), new_start - old_start, old_ref[0, dp + 1] - old_start, new_ref[0, dp + 1] - new_start


def back_by(rows, by):
    return pltpu.roll(rows, lax.rem(128 - by, 128), 0)[:CAP]


def place_kernel(order_ref, old_ref, new_ref, *refs):
    states, arrived_ref, outs = refs[:3], refs[3], refs[4:]
    _, moved, old_count, _ = bounds_of(order_ref, old_ref, new_ref)
    width = arrived_ref.shape[1]
    slots = lax.broadcasted_iota(jnp.int32, (128, width), 0)
    pad = jnp.zeros((128 - CAP, width), F32)
    for k, (ref, out) in enumerate(zip(states, outs)):
        extra = jnp.concatenate([arrived_ref[k * HALO : (k + 1) * HALO, :], jnp.zeros((128 - HALO, width), F32)], axis=0)
        extra = pltpu.roll(extra, old_count, 0)
        out[...] = back_by(jnp.where(slots < old_count, jnp.concatenate([ref[0], pad], axis=0), extra), moved)


def adam_kernel(order_ref, old_ref, new_ref, grad_ref, up_ref, down_ref, master_ref, first_ref, second_ref, *outs):
    new_master, new_first, new_second = outs
    offset, _, _, new_count = bounds_of(order_ref, old_ref, new_ref)
    width = grad_ref.shape[1]
    pad = jnp.zeros((128 - CAP, width), F32)
    grad = back_by(jnp.concatenate([up_ref[...], grad_ref[...], down_ref[...], pad], axis=0), offset) / 8.0
    valid = lax.broadcasted_iota(jnp.int32, (CAP, width), 0) < new_count
    first = beta_one * first_ref[...] + (1.0 - beta_one) * grad
    new_first[0] = jnp.where(valid, first, 0.0)
    second = beta_two * second_ref[...] + (1.0 - beta_two) * grad * grad
    new_second[0] = jnp.where(valid, second, 0.0)
    corr_one = 1.0 - beta_one**adam_step
    corr_two = 1.0 - beta_two**adam_step
    update = first / corr_one / (jnp.sqrt(second / corr_two) + adam_eps)
    master = master_ref[...]
    new_master[0] = jnp.where(valid, master - learn_rate * (update + weight_decay * master), 0.0)


def share_call(kernel, tile, in_specs, out_specs, out_shape, name):
    width = 2 * HALF
    return pl.pallas_call(
        kernel,
        grid_spec=pltpu.PrefetchScalarGridSpec(
            num_scalar_prefetch=3, grid=(width // tile,), in_specs=in_specs, out_specs=out_specs
        ),
        out_shape=out_shape,
        compiler_params=params(GRANT),
        cost_estimate=cost(6),
        name=name,
    )


def place(scalars, states, arrived):
    tile = 1024
    state = pl.BlockSpec((1, CAP, tile), lambda i, *_: (0, 0, i))
    part = lambda n: pl.BlockSpec((n, tile), lambda i, *_: (0, i))
    out = jax.ShapeDtypeStruct(states[0].shape[1:], F32)
    return share_call(place_kernel, tile, [state] * 3 + [part(3 * HALO)], [part(CAP)] * 3, [out] * 3, "place")(
        *scalars, *states, arrived
    )


def adam(scalars, grad, up, down, placed):
    tile = 1024
    state = pl.BlockSpec((1, CAP, tile), lambda i, *_: (0, 0, i))
    part = lambda n: pl.BlockSpec((n, tile), lambda i, *_: (0, i))
    out = jax.ShapeDtypeStruct((1, *placed[0].shape), F32)
    in_specs = [part(64), part(HALO), part(HALO)] + [part(CAP)] * 3
    return share_call(adam_kernel, tile, in_specs, [state] * 3, [out] * 3, "adam")(*scalars, grad, up, down, *placed)


def local(
    cotangent,
    mixer_out,
    gate,
    norm_gain,
    out_weight,
    old_master,
    old_first,
    old_second,
    old_bounds,
    new_bounds,
):
    dp = lax.axis_index("dp")
    tensor = lax.axis_index("tensor")
    x, zl = dp % 4, dp // 4
    y, zh, core = tensor // 4, (tensor // 2) % 2, tensor % 2
    tokens, channels = mixer_out.shape
    blocks = tokens // BLOCK

    order = jnp.stack(
        [
            ((y + dy) % N_Y * 2 + (zh + dz) % 2) * 2 + (core + dc) % 2
            for group in (EARLY, MIDDLE, LATE)
            for dc in (0, 1)
            for dy, dz in group
        ]
        + [x, zl]
    ).astype(jnp.int32)

    row_spec = pl.BlockSpec((4, 1, BLOCK), lambda i: (i, 0, 0))
    block_spec = pl.BlockSpec((4 * BLOCK, channels), lambda i: (i, 0))
    rows_shape = jax.ShapeDtypeStruct((blocks, 1, BLOCK), F32)

    def chip_total(part):
        return part + move(part, TO_CORE)

    def group_total(part):
        return part + move(part, TO_ZHI)

    squares = pl.pallas_call(
        square_kernel,
        grid=(blocks // 4,),
        in_specs=[block_spec, block_spec],
        out_specs=row_spec,
        out_shape=rows_shape,
        compiler_params=params(60),
        cost_estimate=cost(3),
        name="squares",
    )(mixer_out, gate)
    raw = squares
    squares = group_total(squares)
    inverse = lax.rsqrt(chip_total(squares) / GROUP + norm_eps)

    gain = norm_gain[None, :]
    there = pl.BlockSpec((BLOCK, channels), lambda i, o: (o[i], 0))
    here = pl.BlockSpec((BLOCK, channels), lambda i, o: (i, 0))
    there_row = pl.BlockSpec((1, 1, BLOCK), lambda i, o: (o[i], 0, 0))
    gain_spec = pl.BlockSpec((1, channels), lambda i, o: (0, 0))

    def ordered(kernel, in_specs, out_specs, out_shape, name, time, scratch=()):
        return pl.pallas_call(
            kernel,
            grid_spec=pltpu.PrefetchScalarGridSpec(
                num_scalar_prefetch=1, grid=(blocks,), in_specs=in_specs, out_specs=out_specs, scratch_shapes=scratch
            ),
            out_shape=out_shape,
            compiler_params=params(16),
            cost_estimate=cost(time),
            name=name,
        )

    hidden = ordered(
        hidden_kernel,
        [there, there, there_row, gain_spec],
        pl.BlockSpec((channels, BLOCK), lambda i, o: (0, i)),
        jax.ShapeDtypeStruct((channels, tokens), BF16),
        "hidden",
        5,
        [pltpu.VMEM((channels, BLOCK), F32)],
    )(order, mixer_out, gate, inverse, gain)

    states = (old_master, old_first, old_second)

    own = cotangent
    own_z = move(own, TO_ZHI)
    own_m, own_p = move(own, TO_YP), move(own, TO_YM)
    own_s = move(own, TO_CORE)
    own_p = tied(own_p, raw)
    far = move(own_m, TO_YP)
    other_p, other_m = move(own_z, TO_YM), move(own_m, TO_ZHI)
    early = [own, own_z, own_m, own_p, own_s, move(own_z, TO_CORE), move(own_m, TO_CORE), move(own_p, TO_CORE)]
    at = 0
    sums = products(early, hidden, out_weight, at)
    at += 8 * BLOCK
    half = BLOCK // 2
    arrived = move(tied(jnp.concatenate([s[0, :HALO] for s in states], axis=0), sums[0]), TO_LAST)
    last_a = move(tied(other_m[:half], sums[0]), TO_YP)
    last_b = move(tied(other_p[half:], sums[0]), TO_YM)
    middle = [far, other_p, other_m, move(far, TO_CORE), move(other_p, TO_CORE), move(other_m, TO_CORE)]
    sums = products(middle, hidden, out_weight, at, sums)
    at += 6 * BLOCK
    last_a, last_b = tied(last_a, sums[0]), tied(last_b, sums[0])
    last = [last_a, last_b, move(last_a, TO_CORE), move(last_b, TO_CORE)]
    *to_x, to_z, mine_a, mine_b, back = late_products(last, hidden, out_weight, at, sums, arrived)
    got_x, got_z = [move(code, pairs) for code, pairs in zip(to_x, TO_X)], move(to_z, TO_ZLO)

    centre = ordered(
        centre_kernel,
        [here, there, there, there_row, gain_spec],
        there_row,
        rows_shape,
        "centre",
        4,
    )(order, back, mixer_out, gate, inverse, gain)
    scalars = (order, old_bounds, new_bounds)
    placed = place(scalars, states, arrived)
    centre = group_total(chip_total(centre)) / GROUP
    send_a, *send_b, keep_a, keep_b = middle_sums(got_x, got_z, mine_a, mine_b, [centre, placed[0]])
    out_shape = jax.ShapeDtypeStruct((tokens, channels), BF16)
    input_grad, gate_grad = ordered(
        grads_kernel,
        [here, there, there, there_row, there_row, gain_spec],
        [there, there],
        [out_shape, out_shape],
        "grads",
        8,
    )(order, back, mixer_out, gate, inverse, centre, gain)

    got_a, got_b = move(send_a, TO_ZLO), [move(code, pairs) for code, pairs in zip(send_b, TO_X)]
    grad, last_rows, first_rows = last_sums(got_a, got_b, keep_a, keep_b, [input_grad])
    made = adam(scalars, grad, move(last_rows, TO_NEXT), move(first_rows, TO_LAST), placed)
    return (*made, input_grad, gate_grad)


def solution(mesh):
    return jax.shard_map(
        local,
        mesh=mesh,
        in_specs=(
            P(("dp", "tensor"), None),
            P("dp", "tensor"),
            P("dp", "tensor"),
            P("tensor"),
            P("tensor", None),
            P("tensor", "dp", None),
            P("tensor", "dp", None),
            P("tensor", "dp", None),
            P("tensor", None),
            P("tensor", None),
        ),
        out_specs=(
            P("tensor", "dp", None),
            P("tensor", "dp", None),
            P("tensor", "dp", None),
            P("dp", "tensor"),
            P("dp", "tensor"),
        ),
        check_vma=False,
    )
```

```python
import jax
import jax.numpy as jnp
from jax import lax
from jax.experimental import pallas as pl
from jax.experimental.pallas import tpu as pltpu
from jax.sharding import PartitionSpec as P

GROUP = 2048

norm_eps = 1e-05
beta_one = 0.9
beta_two = 0.95
adam_eps = 1e-08
learn_rate = 0.0003
weight_decay = 0.1
adam_step = 1000.0

N_X, N_Y = 4, 4
AXES = ("dp", "tensor")
TILE = 1024
TOP, FINE = 32700.0, 256.0
BLOCK = 128
HALO = 16
CAP = 96
OWNERS = ((1, 0), (1, 1), (3, 0), (3, 1), (2, 0), (2, 1), (0, 0), (0, 1))
HALF = 2048
GRANT = 24
EARLY = ((0, 0), (0, 1), (3, 0), (1, 0))
MIDDLE = ((2, 0), (1, 1), (3, 1))
LATE = ((2, 1),)
F32 = jnp.float32
BF16 = jnp.bfloat16


def position(flat):
    dp, tensor = flat // 16, flat % 16
    return dp % 4, tensor // 4, dp // 4, (tensor // 2) % 2, tensor % 2


def flat_of(x, y, zl, zh, c):
    return (zl * 4 + x) * 16 + (y * 2 + zh) * 2 + c


def pairs_of(move):
    return [(i, flat_of(*move(*position(i)))) for i in range(128)]


TO_CORE = pairs_of(lambda x, y, zl, zh, c: (x, y, zl, zh, 1 - c))
TO_ZHI = pairs_of(lambda x, y, zl, zh, c: (x, y, zl, 1 - zh, c))
TO_YP = pairs_of(lambda x, y, zl, zh, c: (x, (y + 1) % N_Y, zl, zh, c))
TO_YM = pairs_of(lambda x, y, zl, zh, c: (x, (y - 1) % N_Y, zl, zh, c))
TO_ZLO = pairs_of(lambda x, y, zl, zh, c: (x, y, 1 - zl, zh, c))
TO_X = [pairs_of(lambda x, y, zl, zh, c: ((x + dx) % N_X, y, zl, zh, c)) for dx in (1, 3, 2)]
TO_NEXT = [(i, i + 16) for i in range(112)]
TO_LAST = [(i + 16, i) for i in range(112)]


def move(value, pairs):
    return lax.ppermute(value, AXES, pairs)


def tied(value, other):
    late = other[(0,) * other.ndim] > 1e38
    return jnp.where(late, jnp.zeros_like(value), value)


def params(mib):
    return pltpu.CompilerParams(vmem_limit_bytes=mib * 2**20)


def cost(time):
    return pl.CostEstimate(flops=0, bytes_accessed=int(time * 3.3e6), transcendentals=0)


def eye():
    rows = lax.broadcasted_iota(jnp.int32, (BLOCK, BLOCK), 0)
    cols = lax.broadcasted_iota(jnp.int32, (BLOCK, BLOCK), 1)
    return rows == cols


def column_of(row):
    return jnp.sum(jnp.where(eye(), jnp.broadcast_to(row, (BLOCK, BLOCK)), 0.0), axis=1, keepdims=True)


def row_of(column):
    return jnp.sum(jnp.where(eye(), jnp.broadcast_to(column, (BLOCK, BLOCK)), 0.0), axis=0, keepdims=True)


def square_kernel(mixer_ref, gate_ref, out_ref):
    gate = gate_ref[...].astype(F32)
    gated = mixer_ref[...].astype(F32) * (gate * jax.nn.sigmoid(gate))
    total = jnp.sum(gated * gated, axis=1, keepdims=True)
    for k in range(out_ref.shape[0]):
        out_ref[k] = row_of(total[k * BLOCK : (k + 1) * BLOCK])


def hidden_kernel(order_ref, mixer_ref, gate_ref, inverse_ref, gain_ref, out_ref, turned):
    gate = gate_ref[...].astype(F32)
    gated = mixer_ref[...].astype(F32) * (gate * jax.nn.sigmoid(gate))
    normed = gated * column_of(inverse_ref[0])
    hidden = normed * gain_ref[...]
    turned[...] = hidden.T
    x, zl = order_ref[16], order_ref[17]
    for k, (dx, dz) in enumerate(OWNERS):
        start = lax.rem(zl + dz, 2) * 256 + lax.rem(x + dx, N_X) * 64
        out_ref[k * 64 : (k + 1) * 64, :] = turned[pl.ds(pl.multiple_of(start, 64), 64), :].astype(BF16)


def centre_kernel(order_ref, back_ref, mixer_ref, gate_ref, inverse_ref, gain_ref, out_ref):
    gate = gate_ref[...].astype(F32)
    gated = mixer_ref[...].astype(F32) * (gate * jax.nn.sigmoid(gate))
    normed = gated * column_of(inverse_ref[0])
    scaled = back_ref[...] * gain_ref[...]
    out_ref[0] = row_of(jnp.sum(scaled * normed, axis=1, keepdims=True))


def grads_kernel(order_ref, back_ref, mixer_ref, gate_ref, inverse_ref, centre_ref, gain_ref, input_ref, gate_out_ref):
    gate = gate_ref[...].astype(F32)
    mixer = mixer_ref[...].astype(F32)
    sig = jax.nn.sigmoid(gate)
    activated = gate * sig
    slope = sig * (1.0 + gate * (1.0 - sig))
    inverse = column_of(inverse_ref[0])
    normed = mixer * activated * inverse
    scaled = back_ref[...] * gain_ref[...]
    gated_back = inverse * (scaled - normed * column_of(centre_ref[0]))
    input_ref[...] = (gated_back * activated).astype(BF16)
    gate_out_ref[...] = (gated_back * mixer * slope).astype(BF16)


def fetches(pieces, cot, sems, n):
    at, made = 0, []
    cols = pl.ds(n * TILE, TILE)
    for piece in pieces:
        rows = piece.shape[0]
        made.append(pltpu.make_async_copy(piece.at[:, cols], cot.at[pl.ds(at, rows), cols], sems.at[n, len(made)]))
        at += rows
    return made


def arrive(pieces, cot, sems, steps, others=()):
    n = pl.program_id(0)

    @pl.when(n == 0)
    def _():
        for copy in others:
            copy.start()
        for k in range(steps):
            for copy in fetches(pieces, cot, sems, k):
                copy.start()
        for copy in others:
            copy.wait()

    for k in range(steps):

        @pl.when(n == k)
        def _():
            for copy in fetches(pieces, cot, sems, k):
                copy.wait()

    return cot[:, pl.ds(pl.multiple_of(n * TILE, TILE), TILE)]


def columns_of(hidden_ref, start, hid, sem):
    return pltpu.make_async_copy(hidden_ref.at[:, pl.ds(start, hid.shape[1])], hid, sem)


def back_step(cot, weight_ref, sums, back_ref, start, sem, steps):
    n = pl.program_id(0)
    part = lax.dot_general(cot, weight_ref[...], (((1,), (1,)), ((), ())), preferred_element_type=F32)

    @pl.when(n == 0)
    def _():
        sums[...] = part

    @pl.when(n > 0)
    def _():
        sums[...] += part

    @pl.when(n == steps - 1)
    def _():
        out = pltpu.make_async_copy(sums, back_ref.at[pl.ds(start, sums.shape[0])], sem)
        out.start()
        out.wait()


def first_kernel(count, start, steps, *refs):
    pieces, (hidden_ref, weight_ref, grad_ref, back_ref, cot, hid, sums, sems, sem) = refs[:count], refs[count:]
    here = arrive(pieces, cot, sems, steps, [columns_of(hidden_ref, start, hid, sem)])
    grad_ref[...] = jnp.dot(hid[...], here, preferred_element_type=F32)
    back_step(here, weight_ref, sums, back_ref, start, sem, steps)


def next_kernel(count, start, steps, *refs):
    pieces = refs[:count]
    hidden_ref, weight_ref, before_ref, _, grad_ref, back_ref, cot, hid, sums, sems, sem = refs[count:]
    here = arrive(pieces, cot, sems, steps, [columns_of(hidden_ref, start, hid, sem)])
    grad_ref[...] = before_ref[...] + jnp.dot(hid[...], here, preferred_element_type=F32)
    back_step(here, weight_ref, sums, back_ref, start, sem, steps)


def scale_of(code):
    return jnp.exp(code * (0.6931471805599453 / FINE))


def encode(rows, out, start, n):
    here = pl.ds(start, rows.shape[0])
    most = jnp.maximum(jnp.max(jnp.abs(rows), axis=1, keepdims=True), 1e-30)
    code = jnp.ceil(jnp.log2(most) * FINE)
    cols = pl.ds(pl.multiple_of(n * TILE, TILE), TILE)
    out[here, cols] = jnp.round(rows * (TOP / scale_of(code))).astype(jnp.int32).astype(jnp.int16)
    lanes = lax.broadcasted_iota(jnp.int32, (rows.shape[0], 128), 1)
    before = jnp.where(n == 0, 0, out[here, HALF:].astype(jnp.int32))
    out[here, HALF:] = jnp.where(lanes == n, code.astype(jnp.int32), before).astype(jnp.int16)


def decode(part_ref, code_ref, n):
    lanes = lax.broadcasted_iota(jnp.int32, code_ref.shape, 1)
    code = jnp.where(lanes == n, code_ref[...].astype(jnp.int32).astype(F32), 0.0)
    scale = scale_of(jnp.sum(code, axis=1, keepdims=True)) / TOP
    return part_ref[...].astype(jnp.int32).astype(F32) * scale


def late_kernel(count, start, steps, *refs):
    pieces = refs[:count]
    hidden_ref, weight_ref, before_ref, _, *to_x, to_z, mine_a, mine_b, back_ref, cot, hid, sums, sems, sem = refs[count:]
    n = pl.program_id(0)
    here = arrive(pieces, cot, sems, steps, [columns_of(hidden_ref, start, hid, sem)])
    back_step(here, weight_ref, sums, back_ref, start, sem, steps)
    grad = before_ref[...] + jnp.dot(hid[...], here, preferred_element_type=F32)

    @pl.when(n < steps // 2)
    def _():
        for k, out in enumerate(to_x):
            encode(grad[k * 128 : (k + 1) * 128], out, 0, n)
        mine_a[...] = grad[384:]

    @pl.when(n >= steps // 2)
    def _():
        for k in range(4):
            encode(grad[k * 128 + 64 : (k + 1) * 128], to_z, k * 64, n - steps // 2)
            mine_b[k * 64 : (k + 1) * 64] = grad[k * 128 : k * 128 + 64]


def middle_kernel(*refs):
    got_a, got_z, (mine_a, mine_b) = refs[:6], refs[6:8], refs[8:10]
    send_a, *send_b, keep_a, keep_b = refs[-6:]
    n = pl.program_id(0)
    total = mine_a[...]
    for k in range(3):
        total += decode(got_a[2 * k], got_a[2 * k + 1], n)
    keep_a[...] = total[:64]
    encode(total[64:], send_a, 0, n)
    total = mine_b[...] + decode(got_z[0], got_z[1], n)
    for k, out in enumerate(send_b):
        encode(total[k * 64 : (k + 1) * 64], out, 0, n)
    keep_b[...] = total[192:]


def sum_kernel(*refs):
    got_a, got_b, (keep_a, keep_b) = refs[:2], refs[2:8], refs[8:10]
    out_ref, up_ref, down_ref = refs[-3:]
    n = pl.program_id(0)
    total_a = keep_a[...] + decode(got_a[0], got_a[1], n)
    total_b = keep_b[...]
    for k in range(3):
        total_b += decode(got_b[2 * k], got_b[2 * k + 1], n)
    for total, start in ((total_a, 0), (total_b, HALF)):
        cols = pl.ds(pl.multiple_of(start + n * TILE, TILE), TILE)
        out_ref[:, cols] = total
        up_ref[:, cols] = total[64 - HALO :]
        down_ref[:, cols] = total[:HALO]


ANYWHERE = pl.BlockSpec(memory_space=pl.ANY)


def wide(rows):
    return pl.BlockSpec((rows, TILE), lambda n: (0, n))


def kept(rows, cols, at=0):
    return pl.BlockSpec((rows, cols), lambda n: (0, at))


def products(pieces, hidden, weight, start, before=None):
    tokens = sum(p.shape[0] for p in pieces)
    channels, width = weight.shape
    steps, count = width // TILE, len(pieces)
    grad = jax.ShapeDtypeStruct((channels, width), F32)
    back = jax.ShapeDtypeStruct((hidden.shape[1], channels), F32)
    kernel = first_kernel if before is None else next_kernel
    return pl.pallas_call(
        lambda *refs: kernel(count, start, steps, *refs),
        grid=(steps,),
        in_specs=[ANYWHERE] * (count + 1) + [wide(channels)] + ([] if before is None else [wide(channels), ANYWHERE]),
        out_specs=[wide(channels), ANYWHERE],
        out_shape=[grad, back],
        input_output_aliases={} if before is None else {count + 2: 0, count + 3: 1},
        scratch_shapes=[
            pltpu.VMEM((tokens, width), BF16),
            pltpu.VMEM((channels, tokens), BF16),
            pltpu.VMEM((tokens, channels), F32),
            pltpu.SemaphoreType.DMA((steps, count)),
            pltpu.SemaphoreType.DMA,
        ],
        compiler_params=params(GRANT),
        cost_estimate=cost(18 if before is None else 16),
        name="products",
    )(*pieces, hidden, weight, *(before or []))


def late_products(pieces, hidden, weight, start, before, arrived):
    tokens = sum(p.shape[0] for p in pieces)
    channels, width = weight.shape
    steps, count = width // TILE, len(pieces)
    half = steps // 2
    code = lambda rows: jax.ShapeDtypeStruct((rows, HALF + 128), jnp.int16)
    full = lambda rows: jax.ShapeDtypeStruct((rows, HALF), F32)
    back = jax.ShapeDtypeStruct(before[1].shape, F32)
    return pl.pallas_call(
        lambda *refs: late_kernel(count, start, steps, *refs[: count + 4], *refs[count + 5 :]),
        grid=(steps,),
        in_specs=[ANYWHERE] * (count + 1) + [wide(channels), wide(channels), ANYWHERE, ANYWHERE],
        out_specs=[kept(128, HALF + 128)] * 3
        + [
            kept(256, HALF + 128),
            pl.BlockSpec((128, TILE), lambda n: (0, jnp.minimum(n, half - 1))),
            pl.BlockSpec((256, TILE), lambda n: (0, jnp.maximum(n - half, 0))),
            ANYWHERE,
        ],
        out_shape=[code(128)] * 3 + [code(256), full(128), full(256), back],
        input_output_aliases={count + 3: 6},
        scratch_shapes=[
            pltpu.VMEM((tokens, width), BF16),
            pltpu.VMEM((channels, tokens), BF16),
            pltpu.VMEM((tokens, channels), F32),
            pltpu.SemaphoreType.DMA((steps, count)),
            pltpu.SemaphoreType.DMA,
        ],
        compiler_params=params(GRANT),
        cost_estimate=cost(9),
        name="late_products",
    )(*pieces, hidden, weight, *before, arrived)


def coded(rows):
    return [wide(rows), kept(rows, 128, HALF // 128)]


def twice(arrays):
    return [a for array in arrays for a in (array, array)]


def middle_sums(got_a, got_z, mine_a, mine_b, after):
    code = jax.ShapeDtypeStruct((64, HALF + 128), jnp.int16)
    keep = jax.ShapeDtypeStruct((64, HALF), F32)
    return pl.pallas_call(
        middle_kernel,
        grid=(HALF // TILE,),
        in_specs=coded(128) * 3 + coded(256) + [wide(128), wide(256)] + [ANYWHERE] * len(after),
        out_specs=[kept(64, HALF + 128)] * 4 + [wide(64)] * 2,
        out_shape=[code] * 4 + [keep] * 2,
        compiler_params=params(GRANT),
        cost_estimate=cost(3),
        name="middle_sums",
    )(*twice(got_a), *twice([got_z]), mine_a, mine_b, *after)


def last_sums(got_a, got_b, keep_a, keep_b, after):
    width = 2 * HALF
    return pl.pallas_call(
        sum_kernel,
        grid=(HALF // TILE,),
        in_specs=coded(64) * 4 + [wide(64)] * 2 + [ANYWHERE] * len(after),
        out_specs=[kept(64, width), kept(HALO, width), kept(HALO, width)],
        out_shape=[jax.ShapeDtypeStruct((rows, width), F32) for rows in (64, HALO, HALO)],
        compiler_params=params(GRANT),
        cost_estimate=cost(3),
        name="last_sums",
    )(*twice([got_a]), *twice(got_b), keep_a, keep_b, *after)


def bounds_of(order_ref, old_ref, new_ref):
    dp = order_ref[17] * 4 + order_ref[16]
    new_start, old_start = new_ref[0, dp], old_ref[0, dp]
    return new_start - (64 * dp - HALO), new_start - old_start, old_ref[0, dp + 1] - old_start, new_ref[0, dp + 1] - new_start


def back_by(rows, by):
    return pltpu.roll(rows, lax.rem(128 - by, 128), 0)[:CAP]


def place_kernel(order_ref, old_ref, new_ref, *refs):
    states, arrived_ref, outs = refs[:3], refs[3], refs[4:]
    _, moved, old_count, _ = bounds_of(order_ref, old_ref, new_ref)
    width = arrived_ref.shape[1]
    slots = lax.broadcasted_iota(jnp.int32, (128, width), 0)
    pad = jnp.zeros((128 - CAP, width), F32)
    for k, (ref, out) in enumerate(zip(states, outs)):
        extra = jnp.concatenate([arrived_ref[k * HALO : (k + 1) * HALO, :], jnp.zeros((128 - HALO, width), F32)], axis=0)
        extra = pltpu.roll(extra, old_count, 0)
        out[...] = back_by(jnp.where(slots < old_count, jnp.concatenate([ref[0], pad], axis=0), extra), moved)


def adam_kernel(order_ref, old_ref, new_ref, grad_ref, up_ref, down_ref, master_ref, first_ref, second_ref, *outs):
    new_master, new_first, new_second = outs
    offset, _, _, new_count = bounds_of(order_ref, old_ref, new_ref)
    width = grad_ref.shape[1]
    pad = jnp.zeros((128 - CAP, width), F32)
    grad = back_by(jnp.concatenate([up_ref[...], grad_ref[...], down_ref[...], pad], axis=0), offset) / 8.0
    valid = lax.broadcasted_iota(jnp.int32, (CAP, width), 0) < new_count
    first = beta_one * first_ref[...] + (1.0 - beta_one) * grad
    new_first[0] = jnp.where(valid, first, 0.0)
    second = beta_two * second_ref[...] + (1.0 - beta_two) * grad * grad
    new_second[0] = jnp.where(valid, second, 0.0)
    corr_one = 1.0 - beta_one**adam_step
    corr_two = 1.0 - beta_two**adam_step
    update = first / corr_one / (jnp.sqrt(second / corr_two) + adam_eps)
    master = master_ref[...]
    new_master[0] = jnp.where(valid, master - learn_rate * (update + weight_decay * master), 0.0)


def share_call(kernel, tile, in_specs, out_specs, out_shape, name):
    width = 2 * HALF
    return pl.pallas_call(
        kernel,
        grid_spec=pltpu.PrefetchScalarGridSpec(
            num_scalar_prefetch=3, grid=(width // tile,), in_specs=in_specs, out_specs=out_specs
        ),
        out_shape=out_shape,
        compiler_params=params(GRANT),
        cost_estimate=cost(6),
        name=name,
    )


def place(scalars, states, arrived):
    tile = 1024
    state = pl.BlockSpec((1, CAP, tile), lambda i, *_: (0, 0, i))
    part = lambda n: pl.BlockSpec((n, tile), lambda i, *_: (0, i))
    out = jax.ShapeDtypeStruct(states[0].shape[1:], F32)
    return share_call(place_kernel, tile, [state] * 3 + [part(3 * HALO)], [part(CAP)] * 3, [out] * 3, "place")(
        *scalars, *states, arrived
    )


def adam(scalars, grad, up, down, placed):
    tile = 1024
    state = pl.BlockSpec((1, CAP, tile), lambda i, *_: (0, 0, i))
    part = lambda n: pl.BlockSpec((n, tile), lambda i, *_: (0, i))
    out = jax.ShapeDtypeStruct((1, *placed[0].shape), F32)
    in_specs = [part(64), part(HALO), part(HALO)] + [part(CAP)] * 3
    return share_call(adam_kernel, tile, in_specs, [state] * 3, [out] * 3, "adam")(*scalars, grad, up, down, *placed)


def local(
    cotangent,
    mixer_out,
    gate,
    norm_gain,
    out_weight,
    old_master,
    old_first,
    old_second,
    old_bounds,
    new_bounds,
):
    dp = lax.axis_index("dp")
    tensor = lax.axis_index("tensor")
    x, zl = dp % 4, dp // 4
    y, zh, core = tensor // 4, (tensor // 2) % 2, tensor % 2
    tokens, channels = mixer_out.shape
    blocks = tokens // BLOCK

    order = jnp.stack(
        [
            ((y + dy) % N_Y * 2 + (zh + dz) % 2) * 2 + (core + dc) % 2
            for group in (EARLY, MIDDLE, LATE)
            for dc in (0, 1)
            for dy, dz in group
        ]
        + [x, zl]
    ).astype(jnp.int32)

    row_spec = pl.BlockSpec((4, 1, BLOCK), lambda i: (i, 0, 0))
    block_spec = pl.BlockSpec((4 * BLOCK, channels), lambda i: (i, 0))
    rows_shape = jax.ShapeDtypeStruct((blocks, 1, BLOCK), F32)

    def chip_total(part):
        return part + move(part, TO_CORE)

    def group_total(part):
        return part + move(part, TO_ZHI)

    squares = pl.pallas_call(
        square_kernel,
        grid=(blocks // 4,),
        in_specs=[block_spec, block_spec],
        out_specs=row_spec,
        out_shape=rows_shape,
        compiler_params=params(60),
        cost_estimate=cost(3),
        name="squares",
    )(mixer_out, gate)
    raw = squares
    squares = group_total(squares)
    inverse = lax.rsqrt(chip_total(squares) / GROUP + norm_eps)

    gain = norm_gain[None, :]
    there = pl.BlockSpec((BLOCK, channels), lambda i, o: (o[i], 0))
    here = pl.BlockSpec((BLOCK, channels), lambda i, o: (i, 0))
    there_row = pl.BlockSpec((1, 1, BLOCK), lambda i, o: (o[i], 0, 0))
    gain_spec = pl.BlockSpec((1, channels), lambda i, o: (0, 0))

    def ordered(kernel, in_specs, out_specs, out_shape, name, time, scratch=()):
        return pl.pallas_call(
            kernel,
            grid_spec=pltpu.PrefetchScalarGridSpec(
                num_scalar_prefetch=1, grid=(blocks,), in_specs=in_specs, out_specs=out_specs, scratch_shapes=scratch
            ),
            out_shape=out_shape,
            compiler_params=params(16),
            cost_estimate=cost(time),
            name=name,
        )

    hidden = ordered(
        hidden_kernel,
        [there, there, there_row, gain_spec],
        pl.BlockSpec((channels, BLOCK), lambda i, o: (0, i)),
        jax.ShapeDtypeStruct((channels, tokens), BF16),
        "hidden",
        5,
        [pltpu.VMEM((channels, BLOCK), F32)],
    )(order, mixer_out, gate, inverse, gain)

    states = (old_master, old_first, old_second)

    own = cotangent
    own_z = move(own, TO_ZHI)
    own_m, own_p = move(own, TO_YP), move(own, TO_YM)
    own_s = move(own, TO_CORE)
    own_p = tied(own_p, raw)
    far = move(own_m, TO_YP)
    other_p, other_m = move(own_z, TO_YM), move(own_m, TO_ZHI)
    early = [own, own_z, own_m, own_p, own_s, move(own_z, TO_CORE), move(own_m, TO_CORE), move(own_p, TO_CORE)]
    at = 0
    sums = products(early, hidden, out_weight, at)
    at += 8 * BLOCK
    half = BLOCK // 2
    arrived = move(tied(jnp.concatenate([s[0, :HALO] for s in states], axis=0), sums[0]), TO_LAST)
    last_a = move(tied(other_m[:half], sums[0]), TO_YP)
    last_b = move(tied(other_p[half:], sums[0]), TO_YM)
    middle = [far, other_p, other_m, move(far, TO_CORE), move(other_p, TO_CORE), move(other_m, TO_CORE)]
    sums = products(middle, hidden, out_weight, at, sums)
    at += 6 * BLOCK
    last_a, last_b = tied(last_a, sums[0]), tied(last_b, sums[0])
    last = [last_a, last_b, move(last_a, TO_CORE), move(last_b, TO_CORE)]
    *to_x, to_z, mine_a, mine_b, back = late_products(last, hidden, out_weight, at, sums, arrived)
    got_x, got_z = [move(code, pairs) for code, pairs in zip(to_x, TO_X)], move(to_z, TO_ZLO)

    centre = ordered(
        centre_kernel,
        [here, there, there, there_row, gain_spec],
        there_row,
        rows_shape,
        "centre",
        4,
    )(order, back, mixer_out, gate, inverse, gain)
    scalars = (order, old_bounds, new_bounds)
    placed = place(scalars, states, arrived)
    centre = group_total(chip_total(centre)) / GROUP
    send_a, *send_b, keep_a, keep_b = middle_sums(got_x, got_z, mine_a, mine_b, [centre, placed[0]])
    out_shape = jax.ShapeDtypeStruct((tokens, channels), BF16)
    input_grad, gate_grad = ordered(
        grads_kernel,
        [here, there, there, there_row, there_row, gain_spec],
        [there, there],
        [out_shape, out_shape],
        "grads",
        8,
    )(order, back, mixer_out, gate, inverse, centre, gain)

    got_a, got_b = move(send_a, TO_ZLO), [move(code, pairs) for code, pairs in zip(send_b, TO_X)]
    grad, last_rows, first_rows = last_sums(got_a, got_b, keep_a, keep_b, [input_grad])
    made = adam(scalars, grad, move(last_rows, TO_NEXT), move(first_rows, TO_LAST), placed)
    return (*made, input_grad, gate_grad)


def solution(mesh):
    return jax.shard_map(
        local,
        mesh=mesh,
        in_specs=(
            P(("dp", "tensor"), None),
            P("dp", "tensor"),
            P("dp", "tensor"),
            P("tensor"),
            P("tensor", None),
            P("tensor", "dp", None),
            P("tensor", "dp", None),
            P("tensor", "dp", None),
            P("tensor", None),
            P("tensor", None),
        ),
        out_specs=(
            P("tensor", "dp", None),
            P("tensor", "dp", None),
            P("tensor", "dp", None),
            P("dp", "tensor"),
            P("dp", "tensor"),
        ),
        check_vma=False,
    )
```
